512 devices in a mesh: dir: 16 (over y, x_lo), space: 32 (over z, x_hi, core).
Axes of the slice: x: 4 (x_hi: 2, x_lo: 2; x = x_hi * 2 + x_lo), y: 8, z: 8, core: 2. Of those that a mesh axis runs over, the one named last changes fastest.
Arguments:
- velocity: float32 [16, 3, 256, 16, 512], P('dir', None, 'space'), may hold values from -6 to 6
- precursor: float32 [16, 3, 256, 512], P('dir', None, 'space'), may hold values from -6 to 6
- rot_map: int32 [16, 256, 512], P('dir', 'space'), may hold values from 0 to 131071, as said below
- facade_cell: int32 [16, 8192], P('dir', 'space'), may hold values from 0 to 65535
- facade_owner: int32 [16, 8192, 1], P('dir', 'space'), may hold values from 0 to 31; in each aligned block of 256 rows (0 to 255, 256 to 511, ..., all dimensions but the last counted through in order) at most 24 rows name the same one
- facade_panel: int32 [16, 8192], P('dir', 'space'), may hold values from 0 to 127
- facade_area: float32 [16, 8192], P('dir', 'space'), may hold values from 0.2 to 2
Outputs:
- velocity_new: float32 [16, 3, 256, 16, 512], P('dir', None, 'space')
- potential: float32 [16, 256, 16, 512], P('dir', 'space')
- panel_force: float32 [16, 4096], P('dir', 'space')
The draws below stay inside these ranges and needn't reach their ends.
Inputs may be any that keep to these rules, and one draw needn't show every extreme that they name: rot_map[d, y, z] = q_d(y) * 512 + z, where q_d is a permutation of the 256 spanwise rows, drawn for each direction. `facade_owner`: among the 256 facade cells of one device at most 24 have the same owner.
All inputs are finite; a program needn't handle non-finite values.
Results may differ from the reference program's by a relative error of at most 0.00002.
Values sent between devices are 32-bit elements; how exact they have to be, the bound alone decides.
A program may use at most 192 MiB of HBM per device.

```python
import math
import jax
import jax.numpy as jnp
import numpy as np
from jax import lax

CY = 8
NZ = 512
NX = 16
ITERS = 20
FAC_DEV = 256
PAN_DEV = 128
DIRS = 16
NY = 256
FACADES = 8192
CAP = 24
N_SPACE = 32


def draw_rot_map(key, part):
    keys = jax.random.split(jax.random.fold_in(key, 17), DIRS)
    orders = jax.vmap(lambda single: jax.random.permutation(single, NY))(keys).astype(jnp.int32)
    return orders[:, :, None] * NZ + jnp.arange(NZ, dtype=jnp.int32)[None, None, :]


def touch_ends(result, rng, smallest, largest):
    longest = result.shape.index(max(result.shape))
    spots = []
    for shift in (0, 1):
        where = [jax.random.randint(jax.random.fold_in(rng, axis), (), 0, length) for axis, length in enumerate(result.shape)]
        where[longest] = (where[longest] + shift) % result.shape[longest]
        spots.append(tuple(where))
    return result.at[spots[0]].set(smallest).at[spots[1]].set(largest)


def block_levels(rng, shape, cuts, low, high):
    gain = 1.0
    for axis_at, shards_of in cuts:
        steps = jax.random.uniform(jax.random.fold_in(jax.random.fold_in(rng, 6), axis_at), (shards_of,), jnp.float32, low / len(cuts), high / len(cuts))
        gain = gain * jnp.repeat(jnp.exp(steps), shape[axis_at] // shards_of).reshape((-1,) + (1,) * (len(shape) - 1 - axis_at))
    return gain


def shared_out(stream_key, own, number, rows, count, top, limit, slope):
    order = jax.random.permutation(stream_key, count)
    packed, usual = shares(count, rows * top, limit, slope, True), shares(count, rows * top, limit, slope, False)
    places = jnp.arange(count)

    def named(sizes, turn):
        used = int((sizes > 0).sum())
        fixed = max(1, used // 4)
        moved = fixed + (places - fixed + turn * (used - fixed)) % max(1, count - fixed)
        return jnp.zeros((count,), jnp.int32).at[order[jnp.where(places < fixed, places, moved)]].set(jnp.asarray(sizes, jnp.int32))

    sizes = jnp.where(number % 4 == 0, named(packed, number // 4), named(usual, number - number // 4 - 1))
    mixed = jax.random.permutation(jax.random.fold_in(own, 3), count)
    donor, receiver = mixed[0:count // 2 * 2:2], mixed[1:count // 2 * 2:2]
    room = jnp.minimum(sizes[donor] - 1, limit - sizes[receiver]) // 2
    room = jnp.where((donor == order[0]) | (receiver == order[0]) | (sizes[receiver] == 0), 0, jnp.maximum(room, 0))
    moved = jax.random.randint(jax.random.fold_in(own, 4), (count // 2,), 0, 1 << 20) % (room + 1)
    sizes = sizes.at[donor].add(-moved).at[receiver].add(moved)
    items = jnp.searchsorted(jnp.cumsum(sizes), jnp.arange(rows * top), side="right").astype(jnp.int32)
    table = items.reshape(top, rows).T
    table = table[jax.random.permutation(jax.random.fold_in(own, 1), rows)]
    turn = jax.random.randint(jax.random.fold_in(own, 2), (rows, 1), 0, top)
    return jnp.take_along_axis(table, (jnp.arange(top)[None, :] + turn) % top, axis=1)


def shares(count, total, limit, skew, full):
    portions = [(1 << 20) // math.isqrt(grade ** skew) + 1 for grade in range(1, count + 1)]
    largest = limit if full else min(limit, max(-(-total // count), total * portions[0] // sum(portions)))
    least = 1 if total - largest >= count - 1 else 0
    counts, spare = [largest] + [least] * (count - 1), total - largest - least * (count - 1)
    while spare > 0:
        free = [i for i in range(1, count) if counts[i] < largest] or [i for i in range(1, count) if counts[i] < limit]
        pool, remaining = sum([portions[i] for i in free]), spare
        for i in free:
            addition = min(limit - counts[i], max(1, remaining * portions[i] // pool), spare)
            counts[i] = counts[i] + addition
            spare = spare - addition
    return np.array(counts)


def scatter_about(rng, extent, spread, bound, pieces=(), kind=jnp.bfloat16):
    entries = jax.random.normal(rng, extent, jnp.float32) * spread
    if len(pieces) > 0:
        entries = block_levels(rng, extent, pieces, -0.22, 0.18) * entries
    return jnp.clip(entries, min=-bound, max=bound).astype(kind)


def setup_inputs(seed: int = 0) -> dict:
    key_of = jax.random.split(jax.random.key(seed), 8)
    velocity = scatter_about(key_of[0], (DIRS, 3, NY, NX, NZ), 1.0, 6.0, ((0, 16), (2, 32)), jnp.float32)
    precursor = scatter_about(key_of[1], (DIRS, 3, NY, NZ), 1.0, 6.0, ((0, 16), (2, 32)), jnp.float32)
    rot_map = draw_rot_map(jax.random.fold_in(key_of[7], 71), 0)
    facade_cell = touch_ends(jax.random.randint(key_of[3], (DIRS, FACADES), 0, CY * NX * NZ), jax.random.fold_in(key_of[3], 1), 0, (CY * NX * NZ) - 1).astype(jnp.int32)
    facade_owner_keys = jax.random.split(jax.random.fold_in(key_of[4], 1), DIRS * FACADES // FAC_DEV)
    facade_owner_turns = jax.random.permutation(jax.random.fold_in(key_of[4], 3), DIRS * FACADES // FAC_DEV)
    facade_owner = jax.vmap(lambda own, number: shared_out(jax.random.fold_in(key_of[4], 2), own, number, FAC_DEV, N_SPACE, 1, CAP, 2))(facade_owner_keys, facade_owner_turns).reshape((DIRS, FACADES, 1))
    facade_panel = touch_ends(jax.random.randint(key_of[5], (DIRS, FACADES), 0, PAN_DEV), jax.random.fold_in(key_of[5], 1), 0, PAN_DEV - 1).astype(jnp.int32)
    facade_area = jnp.clip(jnp.exp(math.log(2.0) - 2.3025851 * jax.random.uniform(key_of[6], (DIRS, FACADES), jnp.float32) ** block_levels(key_of[6], (DIRS, FACADES), ((0, 16), (1, 32)), -0.2, 0.2)), 0.2, 2.0)
    return {"velocity": velocity, "precursor": precursor, "rot_map": rot_map, "facade_cell": facade_cell, "facade_owner": facade_owner, "facade_panel": facade_panel, "facade_area": facade_area}


time_step = 0.12
viscosity = 0.2


def pad_edges(field):
    lead = field.ndim - 3
    widths = [(0, 0)] * lead
    padded = jnp.pad(field, widths + [(0, 0), (0, 0), (1, 1)])
    return jnp.pad(padded, widths + [(0, 0), (1, 1), (0, 0)], mode="edge")


def tentative(extended):
    q = pad_edges(extended)
    centre = q[:, 1:-1, 1:-1, 1:-1]
    xplus = q[:, 1:-1, 2:, 1:-1]
    xminus = q[:, 1:-1, :-2, 1:-1]
    zplus = q[:, 1:-1, 1:-1, 2:]
    zminus = q[:, 1:-1, 1:-1, :-2]
    yplus = q[:, 2:, 1:-1, 1:-1]
    yminus = q[:, :-2, 1:-1, 1:-1]
    lap = xplus + xminus + zplus + zminus + 16.0 * (yplus + yminus) - 36.0 * centre
    advect = centre[0] * (xplus - xminus) * 0.5 + centre[1] * (yplus - yminus) * 2.0 + centre[2] * (zplus - zminus) * 0.5
    return centre + time_step * (viscosity * lap - advect)


def divergence(extended):
    q = pad_edges(extended)
    along_x = (q[0, 1:-1, 2:, 1:-1] - q[0, 1:-1, :-2, 1:-1]) * 0.5
    along_y = (q[1, 2:, 1:-1, 1:-1] - q[1, :-2, 1:-1, 1:-1]) * 2.0
    along_z = (q[2, 1:-1, 1:-1, 2:] - q[2, 1:-1, 1:-1, :-2]) * 0.5
    return along_x + along_y + along_z


def relax_sweep(extended, source):
    q = jnp.pad(extended, ((0, 0), (1, 1), (1, 1)))
    total = q[1:-1, 2:, 1:-1] + q[1:-1, :-2, 1:-1] + q[1:-1, 1:-1, 2:] + q[1:-1, 1:-1, :-2]
    total = total + 16.0 * (q[2:, 1:-1, 1:-1] + q[:-2, 1:-1, 1:-1])
    return (total - source) / 36.0


def gradient(extended):
    q = jnp.pad(extended, ((0, 0), (1, 1), (1, 1)))
    grad_x = (q[1:-1, 2:, 1:-1] - q[1:-1, :-2, 1:-1]) * 0.5
    grad_y = (q[2:, 1:-1, 1:-1] - q[:-2, 1:-1, 1:-1]) * 2.0
    grad_z = (q[1:-1, 1:-1, 2:] - q[1:-1, 1:-1, :-2]) * 0.5
    return jnp.stack([grad_x, grad_y, grad_z])


def reference(velocity, precursor, rot_map, facade_cell, facade_owner, facade_panel, facade_area):
    plane = precursor[0].reshape(3, NY * NZ)

    def one_direction(items):
        field, rotation, cells, owners, panels, areas = items
        inflow = plane[:, rotation.reshape(-1)].reshape(3, NY, NZ)
        u = field.at[:, :, 0, :].set(inflow)
        ustar = tentative(jnp.pad(u, ((0, 0), (1, 1), (0, 0), (0, 0))))
        source = divergence(jnp.pad(ustar, ((0, 0), (1, 1), (0, 0), (0, 0))))
        phi = jnp.zeros((NY, NX, NZ), jnp.float32)
        for sweep in range(ITERS):
            phi = relax_sweep(jnp.pad(phi, ((1, 1), (0, 0), (0, 0))), source)
        moved = ustar - gradient(jnp.pad(phi, ((1, 1), (0, 0), (0, 0))))
        blocks = phi.reshape(N_SPACE, CY * NX * NZ)
        owner_dev = (jnp.arange(FAC_DEV * N_SPACE) // FAC_DEV).astype(jnp.int32)
        values = areas * blocks[owner_dev, cells]
        target = owners[:, 0] * PAN_DEV + panels
        force = jax.ops.segment_sum(values, target, num_segments=PAN_DEV * N_SPACE)
        return moved, phi, force

    return lax.map(one_direction, (velocity, rot_map, facade_cell, facade_owner, facade_panel, facade_area))
```

```python
import math

import jax
import jax.numpy as jnp
import numpy as np
from jax import lax
from jax.experimental import pallas as pl
from jax.experimental.pallas import tpu as pltpu
from jax.sharding import PartitionSpec as P

ITERS = 20
PAN_DEV = 128
ROWS = 8
NX = 16
NZ = 512
NY = 256
GROUP = 32
LEVELS = 8
DIRS = 16
QUARTER = 128
TILES = 12
HALO = 20
WINDOW = 32 + 2 * HALO
FACADES = 256

time_step = 0.12
viscosity = 0.2

MESH = pl.DeviceIdType.MESH
EXACT = lax.Precision.HIGHEST


def sine_matrix(n):
    k = np.arange(1, n + 1)
    return np.sqrt(2.0 / (n + 1)) * np.sin(np.pi * np.outer(k, k) / (n + 1))


def sweep_taps():
    along_x = 2.0 * np.cos(np.pi * np.arange(1, NX + 1) / (NX + 1))
    along_z = 2.0 * np.cos(np.pi * np.arange(1, NZ + 1) / (NZ + 1))
    own = (along_x[:, None] + along_z[None, :]) / 36.0
    side = 16.0 / 36.0
    width = ITERS
    taps = np.zeros((2 * width + 1, NX, NZ))
    for _ in range(ITERS):
        moved = own * taps
        moved[1:] += side * taps[:-1]
        moved[:-1] += side * taps[1:]
        moved[width] -= 1.0 / 36.0
        taps = moved
    taps = taps[width : width + ITERS]
    return np.stack([taps[:, :, QUARTER * k : QUARTER * (k + 1)] for k in range(4)])


def remote(src, dst, send, recv, to):
    return pltpu.make_async_remote_copy(
        src_ref=src, dst_ref=dst, send_sem=send, recv_sem=recv, device_id=to, device_id_type=MESH
    )


def shift_lanes(q, by):
    lane = lax.broadcasted_iota(jnp.int32, q.shape, 1)
    if by == 1:
        return jnp.where(lane == NZ - 1, 0.0, pltpu.roll(q, NZ - 1, 1))
    return jnp.where(lane == 0, 0.0, pltpu.roll(q, 1, 1))


def shift_x(q, by, edge):
    row = lax.broadcasted_iota(jnp.int32, q.shape, 0)
    if by == 1:
        return jnp.where(row == NX - 1, edge(q), pltpu.roll(q, NX - 1, 0))
    return jnp.where(row == 0, edge(q), pltpu.roll(q, 1, 0))


def copied(q):
    return q


def empty(q):
    return 0.0


def dot(a, b):
    return lax.dot_general(a, b, (((1,), (0,)), ((), ())), precision=EXACT, preferred_element_type=jnp.float32)


def kernel(
    vel, prec, rot, fcell, fown, fpan, farea, sz_hbm, taps_hbm, kx, kx10,
    vout, pout, fout,
    uext, pb, rr, col, pbuf, infl, ust, sz, taps, xh, win, ph, bk, phi, fterm, frecv,
    selrow, colz, colp, cola, ohown,
    load_sem, s_u, r_u, s_p, r_p, s_r, r_r, s_t, r_t, s_i, r_i, s_x, r_x, s_b, r_b, s_f, r_f, l_p,
):
    d = lax.axis_index("dir")
    s = lax.axis_index("space")
    zc = s // 4
    j = s % 4
    chip = s // 2
    is_owner = (s % 2 == 0) & (chip % 4 != 3)
    my_tile = chip - chip // 4
    owners = [2 * (t + t // 3) for t in range(TILES)]

    load_u = pltpu.make_async_copy(vel.at[0], uext.at[:, pl.ds(2, ROWS)], load_sem.at[0])
    load_u.start()
    load_s = pltpu.make_async_copy(sz_hbm, sz, load_sem.at[1])
    load_s.start()
    load_t = pltpu.make_async_copy(taps_hbm.at[j], taps, load_sem.at[2])
    load_t.start()

    barrier = pltpu.get_barrier_semaphore()
    for k in range(1, GROUP):
        pl.semaphore_signal(barrier, inc=1, device_id=(d, (s + k) % GROUP), device_id_type=MESH)

    @pl.when(d != 0)
    def _():
        pl.semaphore_signal(barrier, inc=1, device_id=(0, s), device_id_type=MESH)
        pl.semaphore_wait(barrier, GROUP - 1)

    @pl.when(d == 0)
    def _():
        pl.semaphore_wait(barrier, GROUP - 1 + DIRS - 1)

    @pl.when(d == 0)
    def _():
        for k in range(1, DIRS):
            remote(prec.at[0], pb, s_p.at[k], r_p, (k, s)).start()

    for t in range(TILES):
        @pl.when(s != owners[t])
        def _(t=t):
            remote(rot.at[0, :, pl.ds(0, 128)], rr.at[pl.ds(8 * s, 8)], s_r, r_r, (d, owners[t])).start()

    up = (d, (s + 1) % GROUP)
    down = (d, (s + GROUP - 1) % GROUP)
    edges = [
        remote(vel.at[0, :, pl.ds(7, 1)], uext.at[:, pl.ds(1, 1)], s_u.at[0], r_u.at[0], up),
        remote(vel.at[0, pl.ds(1, 1), pl.ds(6, 1)], uext.at[pl.ds(1, 1), pl.ds(0, 1)], s_u.at[1], r_u.at[1], up),
        remote(vel.at[0, :, pl.ds(0, 1)], uext.at[:, pl.ds(10, 1)], s_u.at[2], r_u.at[2], down),
        remote(vel.at[0, pl.ds(1, 1), pl.ds(1, 1)], uext.at[pl.ds(1, 1), pl.ds(11, 1)], s_u.at[3], r_u.at[3], down),
    ]
    for edge in edges:
        edge.start()

    def column(row):
        return jnp.transpose(jnp.broadcast_to(row, (128, FACADES)))

    cell = column(fcell[...])
    lane = lax.broadcasted_iota(jnp.int32, (FACADES, 128), 1)
    selrow[...] = jnp.where((cell >> 9) == lane, 1.0, 0.0)
    colz[...] = cell & 511
    colp[...] = column(fpan[...])
    cola[...] = column(farea[...])
    ohown[...] = jnp.where(
        lax.broadcasted_iota(jnp.int32, (GROUP, FACADES), 0) == jnp.broadcast_to(fown[...], (GROUP, FACADES)), 1.0, 0.0
    )

    @pl.when(d == 0)
    def _():
        own = pltpu.make_async_copy(prec.at[0], pb, l_p)
        own.start()
        own.wait()

    @pl.when(d != 0)
    def _():
        remote(prec.at[0], pb, s_p.at[0], r_p, (0, s)).wait_recv()

    for t in range(TILES):
        c, k = t // 4, t % 4

        @pl.when(s != owners[t])
        def _(t=t, c=c, k=k):
            remote(pb.at[c, :, pl.ds(128 * k, 128)], col.at[pl.ds(8 * s, 8)], s_t, r_t, (d, owners[t])).start()

        @pl.when(s == owners[t])
        def _(t=t, c=c, k=k):
            col[pl.ds(pl.multiple_of(8 * s, 8), 8), :] = pb[c, :, 128 * k : 128 * (k + 1)]
            rr[pl.ds(pl.multiple_of(8 * s, 8), 8), :] = rot[0, :, 0:128]

    @pl.when(is_owner)
    def _():
        part = pl.ds(0, 8 * (GROUP - 1))
        remote(rr.at[part], rr.at[part], s_r, r_r, (d, (s + 1) % GROUP)).wait_recv()
        q = rr[...] >> 9
        lane = lax.broadcasted_iota(jnp.int32, (NY, 128), 1)
        low = jnp.where(q == lane, 1.0, 0.0)
        high = jnp.where(q - 128 == lane, 1.0, 0.0)
        pbuf[0:8, :] = jnp.zeros((8, 128), jnp.float32)
        pbuf[NY : NY + 8, :] = jnp.zeros((8, 128), jnp.float32)
        remote(col.at[part], col.at[part], s_t, r_t, (d, (s + 1) % GROUP)).wait_recv()
        pbuf[4 : NY + 4, :] = dot(low, col[0:128, :]) + dot(high, col[128:256, :])

        def send(k, carry):
            to = (s + k) % GROUP
            remote(pbuf.at[pl.ds(8 * to, 16)], infl.at[my_tile], s_i, r_i, (d, to)).start()
            return carry

        lax.fori_loop(1, GROUP, send, 0)
        infl[my_tile] = pbuf[pl.ds(pl.multiple_of(8 * s, 8), 16), :]

    load_u.wait()
    for edge in edges:
        edge.wait()

    @pl.when(is_owner)
    def _():
        part = pl.ds(0, TILES - 1)
        remote(infl.at[part], infl.at[part], s_i, r_i, (d, (s + 1) % GROUP)).wait_recv()

    @pl.when(jnp.logical_not(is_owner))
    def _():
        remote(infl, infl, s_i, r_i, (d, (s + 1) % GROUP)).wait_recv()

    for t in range(TILES):
        c, k = t // 4, t % 4
        for r in range(ROWS + 4):
            uext[c, r, 0:1, 128 * k : 128 * (k + 1)] = infl[t, r + 2 : r + 3, :]

    blank = jnp.zeros((2, NX, NZ), jnp.float32)

    @pl.when(s == 0)
    def _():
        for c in range(3):
            uext[c, 0:2] = blank

    @pl.when(s == GROUP - 1)
    def _():
        for c in range(3):
            uext[c, 10:12] = blank

    def tentative(c, r):
        q = uext[c, r]
        yplus = uext[c, r + 1]
        yminus = uext[c, r - 1]
        xplus, xminus = shift_x(q, 1, copied), shift_x(q, -1, copied)
        zplus, zminus = shift_lanes(q, 1), shift_lanes(q, -1)
        lap = xplus + xminus + zplus + zminus + 16.0 * (yplus + yminus) - 36.0 * q
        advect = (
            uext[0, r] * (xplus - xminus) * 0.5
            + uext[1, r] * (yplus - yminus) * 2.0
            + uext[2, r] * (zplus - zminus) * 0.5
        )
        ust[c, r - 1] = q + time_step * (viscosity * lap - advect)

    def row_y(r, carry):
        tentative(1, r)
        return carry

    def row_xz(r, carry):
        tentative(0, r)
        tentative(2, r)
        return carry

    lax.fori_loop(1, ROWS + 3, row_y, 0)
    lax.fori_loop(2, ROWS + 2, row_xz, 0)

    @pl.when(s == 0)
    def _():
        ust[1, 0] = jnp.zeros((NX, NZ), jnp.float32)

    @pl.when(s == GROUP - 1)
    def _():
        ust[1, ROWS + 1] = jnp.zeros((NX, NZ), jnp.float32)

    def row_div(r, carry):
        qx = ust[0, r + 1]
        qz = ust[2, r + 1]
        along_x = (shift_x(qx, 1, copied) - shift_x(qx, -1, copied)) * 0.5
        along_y = (ust[1, r + 2] - ust[1, r]) * 2.0
        along_z = (shift_lanes(qz, 1) - shift_lanes(qz, -1)) * 0.5
        phi[r] = along_x + along_y + along_z
        return carry

    lax.fori_loop(0, ROWS, row_div, 0)

    load_s.wait()
    modes = dot(dot(kx[...], phi[0:ROWS].reshape(ROWS * NX, NZ)), sz[...])
    for k in range(4):
        xh[k] = modes[:, 128 * k : 128 * (k + 1)].reshape(ROWS, NX, QUARTER)

    for dk in range(1, 4):
        k = (j + dk) % 4
        remote(xh.at[k], win.at[pl.ds(HALO + 8 * j, 8)], s_x, r_x, (d, 4 * zc + k)).start()
    above = 4 * ((zc + 1) % LEVELS)
    below = 4 * ((zc + LEVELS - 1) % LEVELS)

    @pl.when(j >= 2)
    def _():
        for k in range(4):
            remote(xh.at[k], win.at[pl.ds(8 * j - 12, 8)], s_x, r_x, (d, above + k)).start()

    @pl.when(j == 1)
    def _():
        for k in range(4):
            remote(xh.at[k, pl.ds(4, 4)], win.at[pl.ds(0, 4)], s_x, r_x, (d, above + k)).start()

    @pl.when(j <= 1)
    def _():
        for k in range(4):
            remote(xh.at[k], win.at[pl.ds(HALO + 32 + 8 * j, 8)], s_x, r_x, (d, below + k)).start()

    @pl.when(j == 2)
    def _():
        for k in range(4):
            remote(xh.at[k, pl.ds(0, 4)], win.at[pl.ds(WINDOW - 4, 4)], s_x, r_x, (d, below + k)).start()

    win[pl.ds(HALO + 8 * j, 8)] = xh[j]
    load_t.wait()
    others = pl.ds(0, WINDOW - 8)
    remote(win.at[others], win.at[others], s_x, r_x, (d, (s + 1) % GROUP)).wait_recv()

    @pl.when(zc == 0)
    def _():
        win[HALO - 1] = jnp.zeros((NX, QUARTER), jnp.float32)
        for i in range(1, HALO):
            win[HALO - 1 - i] = -win[HALO - 1 + i]

    @pl.when(zc == LEVELS - 1)
    def _():
        win[HALO + 32] = jnp.zeros((NX, QUARTER), jnp.float32)
        for i in range(1, HALO):
            win[HALO + 32 + i] = -win[HALO + 32 - i]

    def filter_row(y, carry):
        total = taps[0] * win[y + 19]
        for i in range(1, ITERS):
            total = total + taps[i] * (win[y + 19 + i] + win[y + 19 - i])
        ph[y] = total
        return carry

    lax.fori_loop(0, 34, filter_row, 0)

    for dk in range(1, 4):
        k = (j + dk) % 4
        remote(ph.at[pl.ds(8 * k, 10)], bk.at[j], s_b, r_b, (d, 4 * zc + k)).start()
    bk[j] = ph[pl.ds(8 * j, 10)]
    back = pl.ds(0, 3)
    remote(bk.at[back], bk.at[back], s_b, r_b, (d, (s + 1) % GROUP)).wait_recv()

    spread = sum(dot(bk[k].reshape(10 * NX, QUARTER), sz[128 * k : 128 * (k + 1), :]) for k in range(4))
    phi[...] = dot(kx10[...], spread).reshape(10, NX, NZ)

    @pl.when(s == 0)
    def _():
        phi[0] = jnp.zeros((NX, NZ), jnp.float32)

    @pl.when(s == GROUP - 1)
    def _():
        phi[ROWS + 1] = jnp.zeros((NX, NZ), jnp.float32)

    lines = dot(selrow[...], phi[1 : ROWS + 1].reshape(ROWS * NX, NZ))
    zlane = lax.broadcasted_iota(jnp.int32, (FACADES, NZ), 1)
    value = jnp.sum(jnp.where(colz[:, 0:1] == zlane, lines, 0.0), axis=1, keepdims=True) * cola[:, 0:1]
    lane = lax.broadcasted_iota(jnp.int32, (FACADES, 128), 1)
    terms = dot(ohown[...], jnp.where(colp[...] == lane, value, 0.0))
    for o in range(GROUP):
        fterm[o] = terms[o : o + 1, :]

    def send_terms(k, carry):
        to = (s + k) % GROUP
        remote(fterm.at[to], frecv.at[s], s_f, r_f, (d, to)).start()
        return carry

    lax.fori_loop(1, GROUP, send_terms, 0)
    frecv[s] = fterm[s]

    def row_out(r, carry):
        q = phi[r + 1]
        vout[0, 0, r] = ust[0, r + 1] - (shift_x(q, 1, empty) - shift_x(q, -1, empty)) * 0.5
        vout[0, 1, r] = ust[1, r + 1] - (phi[r + 2] - phi[r]) * 2.0
        vout[0, 2, r] = ust[2, r + 1] - (shift_lanes(q, 1) - shift_lanes(q, -1)) * 0.5
        pout[0, r] = q
        return carry

    lax.fori_loop(0, ROWS, row_out, 0)

    @pl.when(d == 0)
    def _():
        for k in range(1, DIRS):
            remote(prec.at[0], pb, s_p.at[k], r_p, (k, s)).wait_send()

    eight = pl.ds(0, 8 * (TILES - 1))

    remote(rr.at[eight], rr.at[eight], s_r, r_r, up).wait_send()
    remote(col.at[eight], col.at[eight], s_t, r_t, up).wait_send()

    @pl.when(jnp.logical_not(is_owner))
    def _():
        remote(rr.at[pl.ds(0, 8)], rr.at[pl.ds(0, 8)], s_r, r_r, up).wait_send()
        remote(col.at[pl.ds(0, 8)], col.at[pl.ds(0, 8)], s_t, r_t, up).wait_send()

    @pl.when(is_owner)
    def _():
        sent = pl.ds(0, GROUP - 1)
        remote(win.at[sent], win.at[sent], s_i, r_i, up).wait_send()

    @pl.when((j == 0) | (j == 3))
    def _():
        remote(win.at[pl.ds(0, 56)], win.at[pl.ds(0, 56)], s_x, r_x, up).wait_send()

    @pl.when((j == 1) | (j == 2))
    def _():
        remote(win, win, s_x, r_x, up).wait_send()

    remote(bk.at[back], bk.at[back], s_b, r_b, up).wait_send()
    rest = pl.ds(0, GROUP - 1)
    remote(frecv.at[rest], frecv.at[rest], s_f, r_f, up).wait()
    fout[...] = jnp.sum(frecv[...], axis=0)


def body(velocity, precursor, rot_map, facade_cell, facade_owner, facade_panel, facade_area):
    f32 = jnp.float32
    across = sine_matrix(NX)
    constants = [
        jnp.asarray(sine_matrix(NZ), f32),
        jnp.asarray(sweep_taps(), f32),
        jnp.asarray(np.kron(np.eye(ROWS), across), f32),
        jnp.asarray(np.kron(np.eye(ROWS + 2), across), f32),
    ]
    far = pl.BlockSpec(memory_space=pl.ANY)
    near = pl.BlockSpec(memory_space=pltpu.VMEM)
    dma = pltpu.SemaphoreType.DMA
    return pl.pallas_call(
        kernel,
        out_shape=(
            jax.ShapeDtypeStruct((1, 3, ROWS, NX, NZ), f32),
            jax.ShapeDtypeStruct((1, ROWS, NX, NZ), f32),
            jax.ShapeDtypeStruct((1, PAN_DEV), f32),
        ),
        in_specs=[far, far, near, near, near, near, near, far, far, near, near],
        out_specs=(near, near, near),
        scratch_shapes=[
            pltpu.VMEM((3, ROWS + 4, NX, NZ), f32),
            pltpu.VMEM((3, ROWS, NZ), f32),
            pltpu.VMEM((NY, 128), jnp.int32),
            pltpu.VMEM((NY, 128), f32),
            pltpu.VMEM((NY + 8, 128), f32),
            pltpu.VMEM((TILES, 16, 128), f32),
            pltpu.VMEM((3, ROWS + 2, NX, NZ), f32),
            pltpu.VMEM((NZ, NZ), f32),
            pltpu.VMEM((ITERS, NX, QUARTER), f32),
            pltpu.VMEM((4, ROWS, NX, QUARTER), f32),
            pltpu.VMEM((WINDOW, NX, QUARTER), f32),
            pltpu.VMEM((34, NX, QUARTER), f32),
            pltpu.VMEM((4, ROWS + 2, NX, QUARTER), f32),
            pltpu.VMEM((ROWS + 2, NX, NZ), f32),
            pltpu.VMEM((GROUP, 1, PAN_DEV), f32),
            pltpu.VMEM((GROUP, 1, PAN_DEV), f32),
            pltpu.VMEM((FACADES, 128), f32),
            pltpu.VMEM((FACADES, 128), jnp.int32),
            pltpu.VMEM((FACADES, 128), jnp.int32),
            pltpu.VMEM((FACADES, 128), f32),
            pltpu.VMEM((GROUP, FACADES), f32),
            dma((3,)), dma((4,)), dma((4,)), dma((DIRS,)),
            dma, dma, dma, dma, dma, dma, dma, dma, dma, dma, dma, dma, dma, dma,
        ],
        compiler_params=pltpu.CompilerParams(
            collective_id=0, has_side_effects=True, vmem_limit_bytes=48 << 20
        ),
    )(
        velocity, precursor, rot_map, facade_cell, facade_owner.reshape(1, FACADES), facade_panel, facade_area, *constants
    )


def solution(mesh):
    return jax.shard_map(
        body,
        mesh=mesh,
        in_specs=(
            P("dir", None, "space", None, None),
            P("dir", None, "space", None),
            P("dir", "space", None),
            P("dir", "space"),
            P("dir", "space", None),
            P("dir", "space"),
            P("dir", "space"),
        ),
        out_specs=(
            P("dir", None, "space", None, None),
            P("dir", "space", None, None),
            P("dir", "space"),
        ),
        check_vma=False,
    )
```

```python
import math

import jax
import jax.numpy as jnp
import numpy as np
from jax import lax
from jax.experimental import pallas as pl
from jax.experimental.pallas import tpu as pltpu
from jax.sharding import PartitionSpec as P

ITERS = 20
PAN_DEV = 128
ROWS = 8
NX = 16
NZ = 512
NY = 256
GROUP = 32
LEVELS = 8
DIRS = 16
QUARTER = 128
TILES = 12
HALO = 24
LATE = 3
WINDOW = 32 + 2 * HALO
FACADES = 256

time_step = 0.12
viscosity = 0.2

MESH = pl.DeviceIdType.MESH
EXACT = lax.Precision.HIGHEST


def sine_matrix(n):
    k = np.arange(1, n + 1)
    return np.sqrt(2.0 / (n + 1)) * np.sin(np.pi * np.outer(k, k) / (n + 1))


def sweep_taps():
    along_x = 2.0 * np.cos(np.pi * np.arange(1, NX + 1) / (NX + 1))
    along_z = 2.0 * np.cos(np.pi * np.arange(1, NZ + 1) / (NZ + 1))
    own = (along_x[:, None] + along_z[None, :]) / 36.0
    side = 16.0 / 36.0
    width = ITERS
    taps = np.zeros((2 * width + 1, NX, NZ))
    for _ in range(ITERS):
        moved = own * taps
        moved[1:] += side * taps[:-1]
        moved[:-1] += side * taps[1:]
        moved[width] -= 1.0 / 36.0
        taps = moved
    taps = taps[width : width + ITERS]
    return np.stack([taps[:, :, QUARTER * k : QUARTER * (k + 1)] for k in range(4)])


def remote(src, dst, send, recv, to):
    return pltpu.make_async_remote_copy(
        src_ref=src, dst_ref=dst, send_sem=send, recv_sem=recv, device_id=to, device_id_type=MESH
    )


def shift_lanes(q, by):
    lane = lax.broadcasted_iota(jnp.int32, q.shape, 1)
    if by == 1:
        return jnp.where(lane == NZ - 1, 0.0, pltpu.roll(q, NZ - 1, 1))
    return jnp.where(lane == 0, 0.0, pltpu.roll(q, 1, 1))


def shift_x(q, by, edge):
    row = lax.broadcasted_iota(jnp.int32, q.shape, 0)
    if by == 1:
        return jnp.where(row == NX - 1, edge(q), pltpu.roll(q, NX - 1, 0))
    return jnp.where(row == 0, edge(q), pltpu.roll(q, 1, 0))


def copied(q):
    return q


def empty(q):
    return 0.0


def dot(a, b):
    return lax.dot_general(a, b, (((1,), (0,)), ((), ())), precision=EXACT, preferred_element_type=jnp.float32)


def kernel(
    vel, prec, rot, fcell_hbm, fown_hbm, fpan_hbm, farea_hbm, sz_hbm, taps_hbm, kx_hbm, kx10_hbm, sx_hbm,
    vout, pout, fout,
    fcell, fown, fpan, farea, kx, kx10, sx,
    near_x, inlet, xl, wl,
    uext, pb, rr, col, pbuf, infl, ust, sz, taps, xh, win, ph, bk, phi, fterm, frecv,
    selrow, colz, colp, cola, ohown,
    load_sem, go, s_u, r_u, s_p, r_p, s_r, r_r, s_t, r_t, s_i, r_i, s_x, r_x, s_l, r_l, s_b, r_b, s_f, r_f, l_p,
):
    d = lax.axis_index("dir")
    s = lax.axis_index("space")
    zc = s // 4
    j = s % 4
    chip = s // 2
    is_owner = (s % 2 == 0) & (chip % 4 != 3)
    my_tile = chip - chip // 4
    owners = [2 * (t + t // 3) for t in range(TILES)]

    load_u = pltpu.make_async_copy(vel.at[0], uext.at[:, pl.ds(2, ROWS)], load_sem.at[0])
    load_u.start()
    load_s = pltpu.make_async_copy(sz_hbm, sz, load_sem.at[1])
    load_s.start()
    load_t = pltpu.make_async_copy(taps_hbm.at[j], taps, load_sem.at[2])
    load_t.start()
    small = [(fcell_hbm, fcell), (fown_hbm, fown), (fpan_hbm, fpan), (farea_hbm, farea), (kx_hbm, kx), (kx10_hbm, kx10), (sx_hbm, sx)]
    small = [pltpu.make_async_copy(a, b, load_sem.at[3 + i]) for i, (a, b) in enumerate(small)]
    for load in small:
        load.start()

    barrier = pltpu.get_barrier_semaphore()

    @pl.when(d == 0)
    def _():
        for k in range(GROUP):
            pl.semaphore_signal(barrier, inc=1, device_id=(1, (s + k) % GROUP), device_id_type=MESH)
        pl.semaphore_wait(barrier, DIRS - 1)
        for k in range(1, DIRS):
            remote(prec.at[0], pb, s_p.at[k], r_p, (k, s)).start()
        own = pltpu.make_async_copy(prec.at[0], pb, l_p)
        own.start()
        own.wait()
        pl.semaphore_wait(go, 1)

    @pl.when(d != 0)
    def _():
        pl.semaphore_signal(barrier, inc=1, device_id=(0, s), device_id_type=MESH)
        for k in range(1, GROUP):
            pl.semaphore_signal(barrier, inc=1, device_id=(d, (s + k) % GROUP), device_id_type=MESH)

    @pl.when(d == 1)
    def _():
        pl.semaphore_wait(barrier, 2 * GROUP - 1)
        pl.semaphore_signal(go, inc=1, device_id=(0, s), device_id_type=MESH)

    @pl.when(d > 1)
    def _():
        pl.semaphore_wait(barrier, GROUP - 1)

    for t in range(TILES):
        @pl.when(s != owners[t])
        def _(t=t):
            remote(rot.at[0, :, pl.ds(0, 128)], rr.at[pl.ds(8 * s, 8)], s_r, r_r, (d, owners[t])).start()

    up = (d, (s + 1) % GROUP)
    down = (d, (s + GROUP - 1) % GROUP)
    edges = [
        remote(vel.at[0, :, pl.ds(7, 1)], uext.at[:, pl.ds(1, 1)], s_u.at[0], r_u.at[0], up),
        remote(vel.at[0, pl.ds(1, 1), pl.ds(6, 1)], uext.at[pl.ds(1, 1), pl.ds(0, 1)], s_u.at[1], r_u.at[1], up),
        remote(vel.at[0, :, pl.ds(0, 1)], uext.at[:, pl.ds(10, 1)], s_u.at[2], r_u.at[2], down),
        remote(vel.at[0, pl.ds(1, 1), pl.ds(1, 1)], uext.at[pl.ds(1, 1), pl.ds(11, 1)], s_u.at[3], r_u.at[3], down),
    ]
    for edge in edges:
        edge.start()

    def column(row):
        return jnp.transpose(jnp.broadcast_to(row, (128, FACADES)))

    for load in small:
        load.wait()
    cell = column(fcell[...])
    lane = lax.broadcasted_iota(jnp.int32, (FACADES, 128), 1)
    selrow[...] = jnp.where((cell >> 9) == lane, 1.0, 0.0)
    colz[...] = cell & 511
    colp[...] = column(fpan[...])
    cola[...] = column(farea[...])
    ohown[...] = jnp.where(
        lax.broadcasted_iota(jnp.int32, (GROUP, FACADES), 0) == jnp.broadcast_to(fown[...], (GROUP, FACADES)), 1.0, 0.0
    )

    @pl.when(d != 0)
    def _():
        remote(prec.at[0], pb, s_p.at[0], r_p, (0, s)).wait_recv()

    for t in range(TILES):
        c, k = t // 4, t % 4

        @pl.when(s != owners[t])
        def _(t=t, c=c, k=k):
            remote(pb.at[c, :, pl.ds(128 * k, 128)], col.at[pl.ds(8 * s, 8)], s_t, r_t, (d, owners[t])).start()

        @pl.when(s == owners[t])
        def _(t=t, c=c, k=k):
            col[pl.ds(pl.multiple_of(8 * s, 8), 8), :] = pb[c, :, 128 * k : 128 * (k + 1)]
            tile = pltpu.make_async_copy(rot.at[0, :, pl.ds(0, 128)], rr.at[pl.ds(8 * s, 8)], l_p)
            tile.start()
            tile.wait()

    load_u.wait()
    for edge in edges:
        edge.wait()
    blank = jnp.zeros((2, NX, NZ), jnp.float32)

    @pl.when(s == 0)
    def _():
        for c in range(3):
            uext[c, 0:2] = blank

    @pl.when(s == GROUP - 1)
    def _():
        for c in range(3):
            uext[c, 10:12] = blank

    def tentative(c, r):
        q = uext[c, r]
        yplus = uext[c, r + 1]
        yminus = uext[c, r - 1]
        xplus, xminus = shift_x(q, 1, copied), shift_x(q, -1, copied)
        zplus, zminus = shift_lanes(q, 1), shift_lanes(q, -1)
        lap = xplus + xminus + zplus + zminus + 16.0 * (yplus + yminus) - 36.0 * q
        advect = (
            uext[0, r] * (xplus - xminus) * 0.5
            + uext[1, r] * (yplus - yminus) * 2.0
            + uext[2, r] * (zplus - zminus) * 0.5
        )
        result = q + time_step * (viscosity * lap - advect)
        ust[c, r - 1] = jnp.where(lax.broadcasted_iota(jnp.int32, (NX, NZ), 0) < 2, 0.0, result)

    def row_y(r, carry):
        tentative(1, r)
        return carry

    def row_xz(r, carry):
        tentative(0, r)
        tentative(2, r)
        return carry

    lax.fori_loop(1, ROWS + 3, row_y, 0)
    lax.fori_loop(2, ROWS + 2, row_xz, 0)

    @pl.when(s == 0)
    def _():
        ust[1, 0] = jnp.zeros((NX, NZ), jnp.float32)

    @pl.when(s == GROUP - 1)
    def _():
        ust[1, ROWS + 1] = jnp.zeros((NX, NZ), jnp.float32)

    def row_div(r, carry):
        qx = ust[0, r + 1]
        qz = ust[2, r + 1]
        along_x = (shift_x(qx, 1, copied) - shift_x(qx, -1, copied)) * 0.5
        along_y = (ust[1, r + 2] - ust[1, r]) * 2.0
        along_z = (shift_lanes(qz, 1) - shift_lanes(qz, -1)) * 0.5
        phi[r] = along_x + along_y + along_z
        return carry

    lax.fori_loop(0, ROWS, row_div, 0)

    load_s.wait()
    modes = dot(dot(kx[...], phi[0:ROWS].reshape(ROWS * NX, NZ)), sz[...])
    for k in range(4):
        xh[k] = modes[:, 128 * k : 128 * (k + 1)].reshape(ROWS, NX, QUARTER)

    above = 4 * ((zc + 1) % LEVELS)
    below = 4 * ((zc + LEVELS - 1) % LEVELS)

    def to_level(src, dst, send, recv):
        for dk in range(1, 4):
            k = (j + dk) % 4
            remote(src.at[k], dst(3 + j), send, recv, (d, 4 * zc + k)).start()

        @pl.when(j >= 1)
        def _():
            for k in range(4):
                remote(src.at[k], dst(j - 1), send, recv, (d, above + k)).start()

        @pl.when(j <= 2)
        def _():
            for k in range(4):
                remote(src.at[k], dst(7 + j), send, recv, (d, below + k)).start()

    to_level(xh, lambda b: win.at[pl.ds(8 * b, 8)], s_x, r_x)

    for c in range(3):
        for x in (1, 2):
            for r in range(ROWS + 4):
                near_x[c, x - 1, r + 2 : r + 3, :] = uext[c, r, x : x + 1, :]

    @pl.when(is_owner)
    def _():
        part = pl.ds(0, 8 * (GROUP - 1))
        remote(rr.at[part], rr.at[part], s_r, r_r, (d, (s + 1) % GROUP)).wait_recv()
        q = rr[...] >> 9
        lane = lax.broadcasted_iota(jnp.int32, (NY, 128), 1)
        low = jnp.where(q == lane, 1.0, 0.0)
        high = jnp.where(q - 128 == lane, 1.0, 0.0)
        pbuf[0:8, :] = jnp.zeros((8, 128), jnp.float32)
        pbuf[NY : NY + 8, :] = jnp.zeros((8, 128), jnp.float32)
        remote(col.at[part], col.at[part], s_t, r_t, (d, (s + 1) % GROUP)).wait_recv()
        pbuf[4 : NY + 4, :] = dot(low, col[0:128, :]) + dot(high, col[128:256, :])

        def send(k, carry):
            to = (s + k) % GROUP
            remote(pbuf.at[pl.ds(8 * to, 16)], infl.at[my_tile], s_i, r_i, (d, to)).start()
            return carry

        lax.fori_loop(1, GROUP, send, 0)
        infl[my_tile] = pbuf[pl.ds(pl.multiple_of(8 * s, 8), 16), :]

    @pl.when(is_owner)
    def _():
        part = pl.ds(0, TILES - 1)
        remote(infl.at[part], infl.at[part], s_i, r_i, (d, (s + 1) % GROUP)).wait_recv()

    @pl.when(jnp.logical_not(is_owner))
    def _():
        remote(infl, infl, s_i, r_i, (d, (s + 1) % GROUP)).wait_recv()

    height = (2 * ROWS, NZ)
    row = lax.broadcasted_iota(jnp.int32, height, 0)
    outside = ((s == 0) & (row == 3)) | ((s == GROUP - 1) & (row == ROWS + 4))

    def y_next(q):
        return pltpu.roll(q, 2 * ROWS - 1, 0)

    def y_last(q):
        return pltpu.roll(q, 1, 0)

    at0 = [jnp.concatenate([infl[4 * c + k] for k in range(4)], axis=1) for c in range(3)]
    at1 = [near_x[c, 0] for c in range(3)]
    for x, (field, ahead, behind) in enumerate(((at0, at1, at0), (at1, [near_x[c, 1] for c in range(3)], at0))):
        for c in range(3):
            q, xplus, xminus = field[c], ahead[c], behind[c]
            yplus, yminus = y_next(q), y_last(q)
            zplus, zminus = shift_lanes(q, 1), shift_lanes(q, -1)
            lap = xplus + xminus + zplus + zminus + 16.0 * (yplus + yminus) - 36.0 * q
            advect = (
                field[0] * (xplus - xminus) * 0.5
                + field[1] * (yplus - yminus) * 2.0
                + field[2] * (zplus - zminus) * 0.5
            )
            result = q + time_step * (viscosity * lap - advect)
            inlet[x, c] = jnp.where(outside, 0.0, result) if c == 1 else result

    def beside(x):
        qy, qz = inlet[x, 1], inlet[x, 2]
        return (y_next(qy) - y_last(qy)) * 2.0 + (shift_lanes(qz, 1) - shift_lanes(qz, -1)) * 0.5

    v0, v1 = inlet[0, 0], inlet[1, 0]
    parts = [(v1 - v0) * 0.5 + beside(0), beside(1) - v0 * 0.5, v1 * -0.5]
    late = dot(jnp.concatenate([part[4:12] for part in parts], axis=0), sz[...])
    for k in range(4):
        xl[k] = late[:, 128 * k : 128 * (k + 1)]
    to_level(xl, lambda b: wl.at[b], s_l, r_l)

    for x in range(2):
        for c in range(3):
            for r in range(ROWS):
                ust[c, r + 1, x : x + 1, :] = inlet[x, c, r + 4 : r + 5, :]

    win[pl.ds(HALO + 8 * j, 8)] = xh[j]
    wl[3 + j] = xl[j]
    load_t.wait()
    others = pl.ds(0, WINDOW - 8)
    remote(win.at[others], win.at[others], s_x, r_x, (d, (s + 1) % GROUP)).wait_recv()
    nine = pl.ds(0, 9)
    remote(wl.at[nine], wl.at[nine], s_l, r_l, (d, (s + 1) % GROUP)).wait_recv()

    def join(b, carry):
        block = wl[b]
        for r in range(ROWS):
            total = win[8 * b + r]
            for x in range(LATE):
                total = total + jnp.broadcast_to(block[8 * x + r : 8 * x + r + 1, :], (NX, QUARTER)) * sx[x]
            win[8 * b + r] = total
        return carry

    lax.fori_loop(0, WINDOW // 8, join, 0)

    @pl.when(zc == 0)
    def _():
        win[HALO - 1] = jnp.zeros((NX, QUARTER), jnp.float32)
        for i in range(1, ITERS):
            win[HALO - 1 - i] = -win[HALO - 1 + i]

    @pl.when(zc == LEVELS - 1)
    def _():
        win[HALO + 32] = jnp.zeros((NX, QUARTER), jnp.float32)
        for i in range(1, ITERS):
            win[HALO + 32 + i] = -win[HALO + 32 - i]

    backs = []
    for dk in (1, 2, 3, 0):
        first = 8 * ((j + dk) % 4)

        def filter_row(y, carry, first=first, dk=dk):
            at = first + y + HALO - 1
            total = taps[0] * win[at]
            for i in range(1, ITERS):
                total = total + taps[i] * (win[at + i] + win[at - i])
            ph[dk, y] = total
            return carry

        lax.fori_loop(0, ROWS + 2, filter_row, 0)
        if dk:
            back = remote(ph.at[dk], bk.at[dk], s_b.at[dk], r_b.at[dk], (d, 4 * zc + (j + dk) % 4))
            back.start()
            backs.append(back)

    def quarter(block, k):
        return dot(block.reshape(10 * NX, QUARTER), sz[pl.ds(pl.multiple_of(128 * k, 128), 128), :])

    spread = quarter(ph[0], j)
    for dk in (1, 2, 3):
        backs[dk - 1].wait_recv()
        spread = spread + quarter(bk[dk], (j + 4 - dk) % 4)
    phi[...] = dot(kx10[...], spread).reshape(10, NX, NZ)

    @pl.when(s == 0)
    def _():
        phi[0] = jnp.zeros((NX, NZ), jnp.float32)

    @pl.when(s == GROUP - 1)
    def _():
        phi[ROWS + 1] = jnp.zeros((NX, NZ), jnp.float32)

    lines = dot(selrow[...], phi[1 : ROWS + 1].reshape(ROWS * NX, NZ))
    zlane = lax.broadcasted_iota(jnp.int32, (FACADES, NZ), 1)
    value = jnp.sum(jnp.where(colz[:, 0:1] == zlane, lines, 0.0), axis=1, keepdims=True) * cola[:, 0:1]
    lane = lax.broadcasted_iota(jnp.int32, (FACADES, 128), 1)
    terms = dot(ohown[...], jnp.where(colp[...] == lane, value, 0.0))
    for o in range(GROUP):
        fterm[o] = terms[o : o + 1, :]

    def send_terms(k, carry):
        to = (s + k) % GROUP
        remote(fterm.at[to], frecv.at[s], s_f, r_f, (d, to)).start()
        return carry

    lax.fori_loop(1, GROUP, send_terms, 0)
    frecv[s] = fterm[s]

    def row_out(r, carry):
        q = phi[r + 1]
        vout[0, 0, r] = ust[0, r + 1] - (shift_x(q, 1, empty) - shift_x(q, -1, empty)) * 0.5
        vout[0, 1, r] = ust[1, r + 1] - (phi[r + 2] - phi[r]) * 2.0
        vout[0, 2, r] = ust[2, r + 1] - (shift_lanes(q, 1) - shift_lanes(q, -1)) * 0.5
        pout[0, r] = q
        return carry

    lax.fori_loop(0, ROWS, row_out, 0)

    @pl.when(d == 0)
    def _():
        for k in range(1, DIRS):
            remote(prec.at[0], pb, s_p.at[k], r_p, (k, s)).wait_send()

    eight = pl.ds(0, 8 * (TILES - 1))

    remote(rr.at[eight], rr.at[eight], s_r, r_r, up).wait_send()
    remote(col.at[eight], col.at[eight], s_t, r_t, up).wait_send()

    @pl.when(jnp.logical_not(is_owner))
    def _():
        remote(rr.at[pl.ds(0, 8)], rr.at[pl.ds(0, 8)], s_r, r_r, up).wait_send()
        remote(col.at[pl.ds(0, 8)], col.at[pl.ds(0, 8)], s_t, r_t, up).wait_send()

    @pl.when(is_owner)
    def _():
        sent = pl.ds(0, GROUP - 1)
        remote(win.at[sent], win.at[sent], s_i, r_i, up).wait_send()

    @pl.when((j == 0) | (j == 3))
    def _():
        remote(win.at[pl.ds(0, 56)], win.at[pl.ds(0, 56)], s_x, r_x, up).wait_send()
        remote(wl.at[pl.ds(0, 7)], wl.at[pl.ds(0, 7)], s_l, r_l, up).wait_send()

    @pl.when((j == 1) | (j == 2))
    def _():
        remote(win, win, s_x, r_x, up).wait_send()
        remote(win.at[pl.ds(0, 8)], win.at[pl.ds(0, 8)], s_x, r_x, up).wait_send()
        remote(wl, wl, s_l, r_l, up).wait_send()
        remote(wl.at[0], wl.at[0], s_l, r_l, up).wait_send()

    for back in backs:
        back.wait_send()
    rest = pl.ds(0, GROUP - 1)
    remote(frecv.at[rest], frecv.at[rest], s_f, r_f, up).wait()
    fout[...] = jnp.sum(frecv[...], axis=0)


def write_out(a, b, c, a_hbm, b_hbm, c_hbm, sem):
    copies = [pltpu.make_async_copy(x, y, sem.at[i]) for i, (x, y) in enumerate(((a, a_hbm), (b, b_hbm), (c, c_hbm)))]
    for copy in copies:
        copy.start()
    for copy in copies:
        copy.wait()


def body(velocity, precursor, rot_map, facade_cell, facade_owner, facade_panel, facade_area):
    f32 = jnp.float32
    across = sine_matrix(NX)
    constants = [
        jnp.asarray(sine_matrix(NZ), f32),
        jnp.asarray(sweep_taps(), f32),
        jnp.asarray(np.kron(np.eye(ROWS), across), f32),
        jnp.asarray(np.kron(np.eye(ROWS + 2), across), f32),
        jnp.asarray(np.broadcast_to(across[:LATE, :, None], (LATE, NX, QUARTER)), f32),
    ]
    far = pl.BlockSpec(memory_space=pltpu.HBM)
    near = pl.BlockSpec(memory_space=pltpu.VMEM)
    dma = pltpu.SemaphoreType.DMA
    result = pl.pallas_call(
        kernel,
        out_shape=(
            jax.ShapeDtypeStruct((1, 3, ROWS, NX, NZ), f32),
            jax.ShapeDtypeStruct((1, ROWS, NX, NZ), f32),
            jax.ShapeDtypeStruct((1, PAN_DEV), f32),
        ),
        in_specs=[far] * 12,
        out_specs=(near, near, near),
        scratch_shapes=[
            pltpu.VMEM((1, FACADES), jnp.int32),
            pltpu.VMEM((1, FACADES), jnp.int32),
            pltpu.VMEM((1, FACADES), jnp.int32),
            pltpu.VMEM((1, FACADES), f32),
            pltpu.VMEM((ROWS * NX, ROWS * NX), f32),
            pltpu.VMEM(((ROWS + 2) * NX, (ROWS + 2) * NX), f32),
            pltpu.VMEM((LATE, NX, QUARTER), f32),
            pltpu.VMEM((3, 2, 2 * ROWS, NZ), f32),
            pltpu.VMEM((2, 3, 2 * ROWS, NZ), f32),
            pltpu.VMEM((4, LATE * ROWS, QUARTER), f32),
            pltpu.VMEM((WINDOW // 8, LATE * ROWS, QUARTER), f32),
            pltpu.VMEM((3, ROWS + 4, NX, NZ), f32),
            pltpu.VMEM((3, ROWS, NZ), f32),
            pltpu.VMEM((NY, 128), jnp.int32),
            pltpu.VMEM((NY, 128), f32),
            pltpu.VMEM((NY + 8, 128), f32),
            pltpu.VMEM((TILES, 16, 128), f32),
            pltpu.VMEM((3, ROWS + 2, NX, NZ), f32),
            pltpu.VMEM((NZ, NZ), f32),
            pltpu.VMEM((ITERS, NX, QUARTER), f32),
            pltpu.VMEM((4, ROWS, NX, QUARTER), f32),
            pltpu.VMEM((WINDOW, NX, QUARTER), f32),
            pltpu.VMEM((4, ROWS + 2, NX, QUARTER), f32),
            pltpu.VMEM((4, ROWS + 2, NX, QUARTER), f32),
            pltpu.VMEM((ROWS + 2, NX, NZ), f32),
            pltpu.VMEM((GROUP, 1, PAN_DEV), f32),
            pltpu.VMEM((GROUP, 1, PAN_DEV), f32),
            pltpu.VMEM((FACADES, 128), f32),
            pltpu.VMEM((FACADES, 128), jnp.int32),
            pltpu.VMEM((FACADES, 128), jnp.int32),
            pltpu.VMEM((FACADES, 128), f32),
            pltpu.VMEM((GROUP, FACADES), f32),
            dma((10,)), pltpu.SemaphoreType.REGULAR, dma((4,)), dma((4,)), dma((DIRS,)),
            dma, dma, dma, dma, dma, dma, dma, dma, dma, dma, dma, dma((4,)), dma((4,)), dma, dma, dma,
        ],
        compiler_params=pltpu.CompilerParams(
            collective_id=0, has_side_effects=True, vmem_limit_bytes=60 << 20
        ),
    )(
        velocity, precursor, rot_map, facade_cell, facade_owner.reshape(1, FACADES), facade_panel, facade_area, *constants
    )
    return pl.pallas_call(
        write_out,
        out_shape=[jax.ShapeDtypeStruct(x.shape, x.dtype) for x in result],
        in_specs=[near] * 3,
        out_specs=[far] * 3,
        scratch_shapes=[dma((3,))],
    )(*result)


def solution(mesh):
    return jax.shard_map(
        body,
        mesh=mesh,
        in_specs=(
            P("dir", None, "space", None, None),
            P("dir", None, "space", None),
            P("dir", "space", None),
            P("dir", "space"),
            P("dir", "space", None),
            P("dir", "space"),
            P("dir", "space"),
        ),
        out_specs=(
            P("dir", None, "space", None, None),
            P("dir", "space", None, None),
            P("dir", "space"),
        ),
        check_vma=False,
    )
```

```python
import math

import jax
import jax.numpy as jnp
import numpy as np
from jax import lax
from jax.experimental import pallas as pl
from jax.experimental.pallas import tpu as pltpu
from jax.sharding import PartitionSpec as P

ITERS = 20
PAN_DEV = 128
ROWS = 8
NX = 16
NZ = 512
NY = 256
GROUP = 32
LEVELS = 8
DIRS = 16
QUARTER = 128
TILES = 12
HALO = 24
LATE = 3
WINDOW = 32 + 2 * HALO
FACADES = 256

time_step = 0.12
viscosity = 0.2

MESH = pl.DeviceIdType.MESH
EXACT = lax.Precision.HIGHEST


def sine_matrix(n):
    k = np.arange(1, n + 1)
    return np.sqrt(2.0 / (n + 1)) * np.sin(np.pi * np.outer(k, k) / (n + 1))


def sweep_taps():
    along_x = 2.0 * np.cos(np.pi * np.arange(1, NX + 1) / (NX + 1))
    along_z = 2.0 * np.cos(np.pi * np.arange(1, NZ + 1) / (NZ + 1))
    own = (along_x[:, None] + along_z[None, :]) / 36.0
    side = 16.0 / 36.0
    width = ITERS
    taps = np.zeros((2 * width + 1, NX, NZ))
    for _ in range(ITERS):
        moved = own * taps
        moved[1:] += side * taps[:-1]
        moved[:-1] += side * taps[1:]
        moved[width] -= 1.0 / 36.0
        taps = moved
    taps = taps[width : width + ITERS]
    return np.stack([taps[:, :, QUARTER * k : QUARTER * (k + 1)] for k in range(4)])


def remote(src, dst, send, recv, to):
    return pltpu.make_async_remote_copy(
        src_ref=src, dst_ref=dst, send_sem=send, recv_sem=recv, device_id=to, device_id_type=MESH
    )


def shift_lanes(q, by):
    lane = lax.broadcasted_iota(jnp.int32, q.shape, 1)
    if by == 1:
        return jnp.where(lane == NZ - 1, 0.0, pltpu.roll(q, NZ - 1, 1))
    return jnp.where(lane == 0, 0.0, pltpu.roll(q, 1, 1))


def shift_x(q, by, edge):
    row = lax.broadcasted_iota(jnp.int32, q.shape, 0)
    if by == 1:
        return jnp.where(row == NX - 1, edge(q), pltpu.roll(q, NX - 1, 0))
    return jnp.where(row == 0, edge(q), pltpu.roll(q, 1, 0))


def copied(q):
    return q


def empty(q):
    return 0.0


def dot(a, b):
    return lax.dot_general(a, b, (((1,), (0,)), ((), ())), precision=EXACT, preferred_element_type=jnp.float32)


def bdot(a, b):
    return lax.dot_general(a, b, (((1,), (0,)), ((), ())), preferred_element_type=jnp.float32)


def thirds(x):
    high = x.astype(jnp.bfloat16)
    rest = x - high.astype(jnp.float32)
    middle = rest.astype(jnp.bfloat16)
    return high, middle, (rest - middle.astype(jnp.float32)).astype(jnp.bfloat16)


def dot_thirds(x, parts):
    n = x.shape[0]
    high, middle, low = thirds(x)
    a = bdot(jnp.concatenate([high, middle, low], axis=0), parts(0))
    b = bdot(jnp.concatenate([high, middle], axis=0), parts(1))
    c = bdot(high, parts(2))
    return a[:n] + ((a[n : 2 * n] + b[:n]) + (a[2 * n :] + (b[n:] + c)))


def kernel(
    vel, prec, rot, fcell_hbm, fown_hbm, fpan_hbm, farea_hbm, sz_hbm, taps_hbm, kx_hbm, kx10_hbm, sx_hbm,
    vel_hbm, pot_hbm, fout,
    vout,
    fcell, fown, fpan, farea, kx, kx10, sx,
    near_x, inlet, xl, wl,
    uext, pb, rr, col, pbuf, infl, ust, sz, taps, xh, win, ph, bk, phi, fterm, frecv,
    fa, fz, onpan, ohown,
    load_sem, go, s_u, r_u, s_p, r_p, s_r, r_r, s_t, r_t, s_i, r_i, s_x, r_x, s_l, r_l, s_b, r_b, s_f, r_f, s_c, r_c, l_p, out_sem,
):
    d = lax.axis_index("dir")
    s = lax.axis_index("space")
    zc = s // 4
    j = s % 4
    chip = s // 2
    is_owner = (s % 2 == 0) & (chip % 4 != 3)
    my_tile = chip - chip // 4
    owners = [2 * (t + t // 3) for t in range(TILES)]

    load_u = pltpu.make_async_copy(vel.at[0], uext.at[:, pl.ds(2, ROWS)], load_sem.at[0])
    load_u.start()
    load_s = pltpu.make_async_copy(sz_hbm, sz, load_sem.at[1])
    load_s.start()
    load_t = pltpu.make_async_copy(taps_hbm.at[j], taps, load_sem.at[2])
    load_t.start()
    lists = [(fcell_hbm, fcell), (fown_hbm, fown), (fpan_hbm, fpan), (farea_hbm, farea)]
    small = [(a, b.at[j]) for a, b in lists] + [(kx_hbm, kx), (kx10_hbm, kx10), (sx_hbm, sx)]
    small = [pltpu.make_async_copy(a, b, load_sem.at[3 + i]) for i, (a, b) in enumerate(small)]
    for load in small:
        load.start()

    barrier = pltpu.get_barrier_semaphore()

    @pl.when(d == 0)
    def _():
        for k in range(GROUP):
            pl.semaphore_signal(barrier, inc=1, device_id=(1, (s + k) % GROUP), device_id_type=MESH)
        pl.semaphore_wait(barrier, DIRS - 1)
        for k in range(1, DIRS):
            remote(prec.at[0], pb, s_p.at[k], r_p, (k, s)).start()
        own = pltpu.make_async_copy(prec.at[0], pb, l_p)
        own.start()
        own.wait()
        pl.semaphore_wait(go, 1)

    @pl.when(d != 0)
    def _():
        pl.semaphore_signal(barrier, inc=1, device_id=(0, s), device_id_type=MESH)
        for k in range(1, GROUP):
            pl.semaphore_signal(barrier, inc=1, device_id=(d, (s + k) % GROUP), device_id_type=MESH)

    @pl.when(d == 1)
    def _():
        pl.semaphore_wait(barrier, 2 * GROUP - 1)
        pl.semaphore_signal(go, inc=1, device_id=(0, s), device_id_type=MESH)

    @pl.when(d > 1)
    def _():
        pl.semaphore_wait(barrier, GROUP - 1)

    for t in range(TILES):
        @pl.when(s != owners[t])
        def _(t=t):
            remote(rot.at[0, :, pl.ds(0, 128)], rr.at[pl.ds(8 * s, 8)], s_r, r_r, (d, owners[t])).start()

    up = (d, (s + 1) % GROUP)
    down = (d, (s + GROUP - 1) % GROUP)
    edges = [
        remote(vel.at[0, :, pl.ds(7, 1)], uext.at[:, pl.ds(1, 1)], s_u.at[0], r_u.at[0], up),
        remote(vel.at[0, pl.ds(1, 1), pl.ds(6, 1)], uext.at[pl.ds(1, 1), pl.ds(0, 1)], s_u.at[1], r_u.at[1], up),
        remote(vel.at[0, :, pl.ds(0, 1)], uext.at[:, pl.ds(10, 1)], s_u.at[2], r_u.at[2], down),
        remote(vel.at[0, pl.ds(1, 1), pl.ds(1, 1)], uext.at[pl.ds(1, 1), pl.ds(11, 1)], s_u.at[3], r_u.at[3], down),
    ]
    for edge in edges:
        edge.start()

    for dk in range(1, 4):
        for a, b in lists:
            remote(a, b.at[j], s_c, r_c, (d, 4 * zc + (j + dk) % 4)).start()

    @pl.when(d != 0)
    def _():
        remote(prec.at[0], pb, s_p.at[0], r_p, (0, s)).wait_recv()

    for t in range(TILES):
        c, k = t // 4, t % 4

        @pl.when(s != owners[t])
        def _(t=t, c=c, k=k):
            remote(pb.at[c, :, pl.ds(128 * k, 128)], col.at[pl.ds(8 * s, 8)], s_t, r_t, (d, owners[t])).start()

        @pl.when(s == owners[t])
        def _(t=t, c=c, k=k):
            col[pl.ds(pl.multiple_of(8 * s, 8), 8), :] = pb[c, :, 128 * k : 128 * (k + 1)]
            tile = pltpu.make_async_copy(rot.at[0, :, pl.ds(0, 128)], rr.at[pl.ds(8 * s, 8)], l_p)
            tile.start()
            tile.wait()

    @pl.when(is_owner)
    def _():
        part = pl.ds(0, 8 * (GROUP - 1))
        remote(rr.at[part], rr.at[part], s_r, r_r, (d, (s + 1) % GROUP)).wait_recv()
        q = rr[...] >> 9
        lane = lax.broadcasted_iota(jnp.int32, (NY, 128), 1)
        chosen = jnp.concatenate([jnp.where(q == lane, 1.0, 0.0), jnp.where(q - 128 == lane, 1.0, 0.0)], axis=1)
        chosen = chosen.astype(jnp.bfloat16)
        pbuf[0:8, :] = jnp.zeros((8, 128), jnp.float32)
        pbuf[NY : NY + 8, :] = jnp.zeros((8, 128), jnp.float32)
        remote(col.at[part], col.at[part], s_t, r_t, (d, (s + 1) % GROUP)).wait_recv()
        rows = bdot(chosen, jnp.concatenate(thirds(col[...]), axis=1))
        pbuf[4 : NY + 4, :] = rows[:, 0:128] + (rows[:, 128:256] + rows[:, 256:384])

        def send(i, carry):
            to = (s + 16 + ((i + 1) // 2) * (2 * (i % 2) - 1)) % GROUP
            remote(pbuf.at[pl.ds(8 * to, 16)], infl.at[my_tile], s_i, r_i, (d, to)).start()
            return carry

        lax.fori_loop(0, GROUP - 1, send, 0)
        infl[my_tile] = pbuf[pl.ds(pl.multiple_of(8 * s, 8), 16), :]

    load_u.wait()
    for load in small:
        load.wait()
    for edge in edges:
        edge.wait()
    blank = jnp.zeros((2, NX, NZ), jnp.float32)

    @pl.when(s == 0)
    def _():
        for c in range(3):
            uext[c, 0:2] = blank

    @pl.when(s == GROUP - 1)
    def _():
        for c in range(3):
            uext[c, 10:12] = blank

    def tentative(c, r):
        q = uext[c, r]
        yplus = uext[c, r + 1]
        yminus = uext[c, r - 1]
        xplus, xminus = shift_x(q, 1, copied), shift_x(q, -1, copied)
        zplus, zminus = shift_lanes(q, 1), shift_lanes(q, -1)
        lap = xplus + xminus + zplus + zminus + 16.0 * (yplus + yminus) - 36.0 * q
        advect = (
            uext[0, r] * (xplus - xminus) * 0.5
            + uext[1, r] * (yplus - yminus) * 2.0
            + uext[2, r] * (zplus - zminus) * 0.5
        )
        result = q + time_step * (viscosity * lap - advect)
        ust[c, r - 1] = jnp.where(lax.broadcasted_iota(jnp.int32, (NX, NZ), 0) < 2, 0.0, result)

    def row_y(r, carry):
        tentative(1, r)
        return carry

    def row_xz(r, carry):
        tentative(0, r)
        tentative(2, r)
        return carry

    lax.fori_loop(1, ROWS + 3, row_y, 0)
    lax.fori_loop(2, ROWS + 2, row_xz, 0)

    @pl.when(s == 0)
    def _():
        ust[1, 0] = jnp.zeros((NX, NZ), jnp.float32)

    @pl.when(s == GROUP - 1)
    def _():
        ust[1, ROWS + 1] = jnp.zeros((NX, NZ), jnp.float32)

    def row_div(r, carry):
        qx = ust[0, r + 1]
        qz = ust[2, r + 1]
        along_x = (shift_x(qx, 1, copied) - shift_x(qx, -1, copied)) * 0.5
        along_y = (ust[1, r + 2] - ust[1, r]) * 2.0
        along_z = (shift_lanes(qz, 1) - shift_lanes(qz, -1)) * 0.5
        phi[r] = along_x + along_y + along_z
        return carry

    lax.fori_loop(0, ROWS, row_div, 0)

    load_s.wait()
    modes = dot_thirds(dot(kx[...], phi[0:ROWS].reshape(ROWS * NX, NZ)), lambda i: sz[i])
    for k in range(4):
        xh[k] = modes[:, 128 * k : 128 * (k + 1)].reshape(ROWS, NX, QUARTER)

    above = 4 * ((zc + 1) % LEVELS)
    below = 4 * ((zc + LEVELS - 1) % LEVELS)

    def to_level(src, dst, send, recv):
        for dk in range(1, 4):
            k = (j + dk) % 4
            remote(src.at[k], dst(3 + j), send, recv, (d, 4 * zc + k)).start()

        @pl.when(j >= 1)
        def _():
            for k in range(4):
                remote(src.at[k], dst(j - 1), send, recv, (d, above + k)).start()

        @pl.when(j <= 2)
        def _():
            for k in range(4):
                remote(src.at[k], dst(7 + j), send, recv, (d, below + k)).start()

    to_level(xh, lambda b: win.at[pl.ds(8 * b, 8)], s_x, r_x)

    for c in range(3):
        for x in (1, 2):
            for r in range(ROWS + 4):
                near_x[c, x - 1, r + 2 : r + 3, :] = uext[c, r, x : x + 1, :]

    @pl.when(is_owner)
    def _():
        part = pl.ds(0, TILES - 1)
        remote(infl.at[part], infl.at[part], s_i, r_i, (d, (s + 1) % GROUP)).wait_recv()

    @pl.when(jnp.logical_not(is_owner))
    def _():
        remote(infl, infl, s_i, r_i, (d, (s + 1) % GROUP)).wait_recv()

    height = (2 * ROWS, NZ)
    row = lax.broadcasted_iota(jnp.int32, height, 0)
    outside = ((s == 0) & (row == 3)) | ((s == GROUP - 1) & (row == ROWS + 4))

    def y_next(q):
        return pltpu.roll(q, 2 * ROWS - 1, 0)

    def y_last(q):
        return pltpu.roll(q, 1, 0)

    at0 = [jnp.concatenate([infl[4 * c + k] for k in range(4)], axis=1) for c in range(3)]
    at1 = [near_x[c, 0] for c in range(3)]
    for x, (field, ahead, behind) in enumerate(((at0, at1, at0), (at1, [near_x[c, 1] for c in range(3)], at0))):
        for c in range(3):
            q, xplus, xminus = field[c], ahead[c], behind[c]
            yplus, yminus = y_next(q), y_last(q)
            zplus, zminus = shift_lanes(q, 1), shift_lanes(q, -1)
            lap = xplus + xminus + zplus + zminus + 16.0 * (yplus + yminus) - 36.0 * q
            advect = (
                field[0] * (xplus - xminus) * 0.5
                + field[1] * (yplus - yminus) * 2.0
                + field[2] * (zplus - zminus) * 0.5
            )
            result = q + time_step * (viscosity * lap - advect)
            inlet[x, c] = jnp.where(outside, 0.0, result) if c == 1 else result

    def beside(x):
        qy, qz = inlet[x, 1], inlet[x, 2]
        return (y_next(qy) - y_last(qy)) * 2.0 + (shift_lanes(qz, 1) - shift_lanes(qz, -1)) * 0.5

    v0, v1 = inlet[0, 0], inlet[1, 0]
    parts = [(v1 - v0) * 0.5 + beside(0), beside(1) - v0 * 0.5, v1 * -0.5]
    rows = [part[4:12] for part in parts] + [jnp.zeros((ROWS, NZ), jnp.float32)]
    late = dot_thirds(jnp.concatenate(rows, axis=0), lambda i: sz[i])
    for k in range(4):
        xl[k] = late[0 : LATE * ROWS, 128 * k : 128 * (k + 1)]
    to_level(xl, lambda b: wl.at[b], s_l, r_l)

    for x in range(2):
        for c in range(3):
            for r in range(ROWS):
                ust[c, r + 1, x : x + 1, :] = inlet[x, c, r + 4 : r + 5, :]

    remote(xl.at[0], xl.at[0], s_c, r_c, up).wait_recv()
    wide = lax.broadcasted_iota(jnp.int32, (FACADES, 128), 1)
    tall = lax.broadcasted_iota(jnp.int32, (FACADES, NZ), 1)
    mine = pl.ds(pl.multiple_of(128 * j, 128), 128)

    def prepare(q, carry):
        cell = jnp.transpose(jnp.broadcast_to(fcell[q], (8, FACADES)))[:, 0:1]
        panel = jnp.transpose(jnp.broadcast_to(fpan[q], (8, FACADES)))[:, 0:1]
        area = jnp.transpose(jnp.broadcast_to(farea[q], (8, FACADES)))[:, 0:1]
        fa[q] = dot(jnp.where((cell >> 9) == wide, 1.0, 0.0), kx[...])
        at = jnp.where((cell & 511) == tall, 1.0, 0.0).astype(jnp.bfloat16)
        fz[q] = (bdot(at, sz[0, :, mine]) + (bdot(at, sz[1, :, mine]) + bdot(at, sz[2, :, mine]))) * area
        onpan[q] = jnp.where(panel == wide, 1.0, 0.0)
        ohown[q] = jnp.where(lax.broadcasted_iota(jnp.int32, (GROUP, FACADES), 0) == fown[q], 1.0, 0.0)
        return carry

    lax.fori_loop(0, 4, prepare, 0)

    win[pl.ds(HALO + 8 * j, 8)] = xh[j]
    wl[3 + j] = xl[j]
    load_t.wait()
    others = pl.ds(0, WINDOW - 8)
    remote(win.at[others], win.at[others], s_x, r_x, (d, (s + 1) % GROUP)).wait_recv()
    nine = pl.ds(0, 9)
    remote(wl.at[nine], wl.at[nine], s_l, r_l, (d, (s + 1) % GROUP)).wait_recv()

    def join(b, carry):
        block = wl[b]
        for r in range(ROWS):
            total = win[8 * b + r]
            for x in range(LATE):
                total = total + jnp.broadcast_to(block[8 * x + r : 8 * x + r + 1, :], (NX, QUARTER)) * sx[x]
            win[8 * b + r] = total
        return carry

    lax.fori_loop(0, WINDOW // 8, join, 0)

    @pl.when(zc == 0)
    def _():
        win[HALO - 1] = jnp.zeros((NX, QUARTER), jnp.float32)
        for i in range(1, ITERS):
            win[HALO - 1 - i] = -win[HALO - 1 + i]

    @pl.when(zc == LEVELS - 1)
    def _():
        win[HALO + 32] = jnp.zeros((NX, QUARTER), jnp.float32)
        for i in range(1, ITERS):
            win[HALO + 32 + i] = -win[HALO + 32 - i]

    backs = []
    for dk in (2, 3, 1, 0):
        first = 8 * (j ^ dk)

        def filter_row(y, carry, first=first, dk=dk):
            at = first + y + HALO - 1
            total = taps[0] * win[at]
            for i in range(1, ITERS):
                total = total + taps[i] * (win[at + i] + win[at - i])
            ph[dk, y] = total
            return carry

        lax.fori_loop(0, ROWS + 2, filter_row, 0)
        if dk:
            back = remote(ph.at[dk], bk.at[dk], s_b.at[dk], r_b.at[dk], (d, 4 * zc + (j ^ dk)))
            back.start()
            backs.append(back)

    terms = jnp.zeros((GROUP, PAN_DEV), jnp.float32)
    for dk in range(4):
        q = j ^ dk
        lines = dot(fa[q], ph[dk, 1 : ROWS + 1].reshape(ROWS * NX, QUARTER))
        value = jnp.sum(lines * fz[q], axis=1, keepdims=True)
        terms = terms + dot(ohown[q], onpan[q] * value)
    for o in range(GROUP):
        fterm[o] = terms[o : o + 1, :]

    def send_terms(i, carry):
        to = (s + 16 + ((i + 1) // 2) * (2 * (i % 2) - 1)) % GROUP
        remote(fterm.at[to], frecv.at[s], s_f, r_f, (d, to)).start()
        return carry

    lax.fori_loop(0, GROUP - 1, send_terms, 0)
    frecv[s] = fterm[s]

    def quarter(block, k):
        rows = pl.ds(pl.multiple_of(128 * k, 128), 128)
        return dot_thirds(block.reshape(10 * NX, QUARTER), lambda i: sz[i, rows, :])

    spread = quarter(ph[0], j)
    for dk in (1, 2, 3):
        arrived = backs[(2, 3, 1).index(dk)]
        arrived.wait_recv()
        spread = spread + quarter(bk[dk], j ^ dk)
    phi[...] = dot(kx10[...], spread).reshape(10, NX, NZ)

    @pl.when(s == 0)
    def _():
        phi[0] = jnp.zeros((NX, NZ), jnp.float32)

    @pl.when(s == GROUP - 1)
    def _():
        phi[ROWS + 1] = jnp.zeros((NX, NZ), jnp.float32)

    def row_out(r, carry):
        q = phi[r + 1]
        vout[0, r] = ust[0, r + 1] - (shift_x(q, 1, empty) - shift_x(q, -1, empty)) * 0.5
        vout[1, r] = ust[1, r + 1] - (phi[r + 2] - phi[r]) * 2.0
        vout[2, r] = ust[2, r + 1] - (shift_lanes(q, 1) - shift_lanes(q, -1)) * 0.5
        return carry

    lax.fori_loop(0, ROWS, row_out, 0)
    outs = [
        pltpu.make_async_copy(phi.at[pl.ds(1, ROWS)], pot_hbm.at[0], out_sem.at[0]),
        pltpu.make_async_copy(vout, vel_hbm.at[0], out_sem.at[1]),
    ]
    for out in outs:
        out.start()

    @pl.when(d == 0)
    def _():
        for k in range(1, DIRS):
            remote(prec.at[0], pb, s_p.at[k], r_p, (k, s)).wait_send()

    eight = pl.ds(0, 8 * (TILES - 1))

    remote(xl.at[0], xl.at[0], s_c, r_c, up).wait_send()
    remote(rr.at[eight], rr.at[eight], s_r, r_r, up).wait_send()
    remote(col.at[eight], col.at[eight], s_t, r_t, up).wait_send()

    @pl.when(jnp.logical_not(is_owner))
    def _():
        remote(rr.at[pl.ds(0, 8)], rr.at[pl.ds(0, 8)], s_r, r_r, up).wait_send()
        remote(col.at[pl.ds(0, 8)], col.at[pl.ds(0, 8)], s_t, r_t, up).wait_send()

    @pl.when(is_owner)
    def _():
        sent = pl.ds(0, GROUP - 1)
        remote(win.at[sent], win.at[sent], s_i, r_i, up).wait_send()

    @pl.when((j == 0) | (j == 3))
    def _():
        remote(win.at[pl.ds(0, 56)], win.at[pl.ds(0, 56)], s_x, r_x, up).wait_send()
        remote(wl.at[pl.ds(0, 7)], wl.at[pl.ds(0, 7)], s_l, r_l, up).wait_send()

    @pl.when((j == 1) | (j == 2))
    def _():
        remote(win, win, s_x, r_x, up).wait_send()
        remote(win.at[pl.ds(0, 8)], win.at[pl.ds(0, 8)], s_x, r_x, up).wait_send()
        remote(wl, wl, s_l, r_l, up).wait_send()
        remote(wl.at[0], wl.at[0], s_l, r_l, up).wait_send()

    for back in backs:
        back.wait_send()
    rest = pl.ds(0, GROUP - 1)
    remote(frecv.at[rest], frecv.at[rest], s_f, r_f, up).wait()
    fout[...] = jnp.sum(frecv[...], axis=0)
    for out in outs:
        out.wait()


def write_out(vel, pot, force, vel_out, pot_out, force_out, vbuf, pbuf, fbuf, into, out):
    half = ROWS // 2
    parts = [
        (vel.at[0, c, pl.ds(r, half)], vbuf.at[c, pl.ds(r, half)], vel_out.at[0, c, pl.ds(r, half)])
        for c in range(3)
        for r in (0, half)
    ]
    parts += [(pot.at[0, pl.ds(r, half)], pbuf.at[pl.ds(r, half)], pot_out.at[0, pl.ds(r, half)]) for r in (0, half)]
    parts.append((force, fbuf, force_out))
    loads = [pltpu.make_async_copy(a, b, into.at[i]) for i, (a, b, _) in enumerate(parts)]
    stores = [pltpu.make_async_copy(b, c, out.at[i]) for i, (_, b, c) in enumerate(parts)]
    for load in loads:
        load.start()
    for load, store in zip(loads, stores):
        load.wait()
        store.start()
    for store in stores:
        store.wait()


def body(velocity, precursor, rot_map, facade_cell, facade_owner, facade_panel, facade_area):
    f32 = jnp.float32
    across = sine_matrix(NX)
    constants = [
        jnp.stack(thirds(jnp.asarray(sine_matrix(NZ), f32))),
        jnp.asarray(sweep_taps(), f32),
        jnp.asarray(np.kron(np.eye(ROWS), across), f32),
        jnp.asarray(np.kron(np.eye(ROWS + 2), across), f32),
        jnp.asarray(np.broadcast_to(across[:LATE, :, None], (LATE, NX, QUARTER)), f32),
    ]
    far = pl.BlockSpec(memory_space=pltpu.HBM)
    near = pl.BlockSpec(memory_space=pltpu.VMEM)
    dma = pltpu.SemaphoreType.DMA
    result = pl.pallas_call(
        kernel,
        out_shape=(
            jax.ShapeDtypeStruct((1, 3, ROWS, NX, NZ), f32),
            jax.ShapeDtypeStruct((1, ROWS, NX, NZ), f32),
            jax.ShapeDtypeStruct((1, PAN_DEV), f32),
        ),
        in_specs=[far] * 12,
        out_specs=(far, far, near),
        scratch_shapes=[
            pltpu.VMEM((3, ROWS, NX, NZ), f32),
            pltpu.VMEM((4, 1, FACADES), jnp.int32),
            pltpu.VMEM((4, 1, FACADES), jnp.int32),
            pltpu.VMEM((4, 1, FACADES), jnp.int32),
            pltpu.VMEM((4, 1, FACADES), f32),
            pltpu.VMEM((ROWS * NX, ROWS * NX), f32),
            pltpu.VMEM(((ROWS + 2) * NX, (ROWS + 2) * NX), f32),
            pltpu.VMEM((LATE, NX, QUARTER), f32),
            pltpu.VMEM((3, 2, 2 * ROWS, NZ), f32),
            pltpu.VMEM((2, 3, 2 * ROWS, NZ), f32),
            pltpu.VMEM((4, LATE * ROWS, QUARTER), f32),
            pltpu.VMEM((WINDOW // 8, LATE * ROWS, QUARTER), f32),
            pltpu.VMEM((3, ROWS + 4, NX, NZ), f32),
            pltpu.VMEM((3, ROWS, NZ), f32),
            pltpu.VMEM((NY, 128), jnp.int32),
            pltpu.VMEM((NY, 128), f32),
            pltpu.VMEM((NY + 8, 128), f32),
            pltpu.VMEM((TILES, 16, 128), f32),
            pltpu.VMEM((3, ROWS + 2, NX, NZ), f32),
            pltpu.VMEM((3, NZ, NZ), jnp.bfloat16),
            pltpu.VMEM((ITERS, NX, QUARTER), f32),
            pltpu.VMEM((4, ROWS, NX, QUARTER), f32),
            pltpu.VMEM((WINDOW, NX, QUARTER), f32),
            pltpu.VMEM((4, ROWS + 2, NX, QUARTER), f32),
            pltpu.VMEM((4, ROWS + 2, NX, QUARTER), f32),
            pltpu.VMEM((ROWS + 2, NX, NZ), f32),
            pltpu.VMEM((GROUP, 1, PAN_DEV), f32),
            pltpu.VMEM((GROUP, 1, PAN_DEV), f32),
            pltpu.VMEM((4, FACADES, 128), f32),
            pltpu.VMEM((4, FACADES, 128), f32),
            pltpu.VMEM((4, FACADES, 128), f32),
            pltpu.VMEM((4, GROUP, FACADES), f32),
            dma((10,)), pltpu.SemaphoreType.REGULAR, dma((4,)), dma((4,)), dma((DIRS,)),
            dma, dma, dma, dma, dma, dma, dma, dma, dma, dma, dma, dma((4,)), dma((4,)), dma, dma, dma, dma, dma, dma((2,)),
        ],
        compiler_params=pltpu.CompilerParams(
            collective_id=0, has_side_effects=True, vmem_limit_bytes=60 << 20
        ),
    )(
        velocity, precursor, rot_map, facade_cell, facade_owner.reshape(1, FACADES), facade_panel, facade_area, *constants
    )
    return pl.pallas_call(
        write_out,
        out_shape=[jax.ShapeDtypeStruct(x.shape, x.dtype) for x in result],
        in_specs=[far] * 3,
        out_specs=[far] * 3,
        scratch_shapes=[
            pltpu.VMEM((3, ROWS, NX, NZ), f32),
            pltpu.VMEM((ROWS, NX, NZ), f32),
            pltpu.VMEM((1, PAN_DEV), f32),
            dma((9,)),
            dma((9,)),
        ],
        compiler_params=pltpu.CompilerParams(vmem_limit_bytes=60 << 20),
    )(*result)


def solution(mesh):
    return jax.shard_map(
        body,
        mesh=mesh,
        in_specs=(
            P("dir", None, "space", None, None),
            P("dir", None, "space", None),
            P("dir", "space", None),
            P("dir", "space"),
            P("dir", "space", None),
            P("dir", "space"),
            P("dir", "space"),
        ),
        out_specs=(
            P("dir", None, "space", None, None),
            P("dir", "space", None, None),
            P("dir", "space"),
        ),
        check_vma=False,
    )
```

```python
import math

import jax
import jax.numpy as jnp
import numpy as np
from jax import lax
from jax.experimental import pallas as pl
from jax.experimental.pallas import tpu as pltpu
from jax.sharding import PartitionSpec as P

ITERS = 20
PAN_DEV = 128
ROWS = 8
NX = 16
NZ = 512
NY = 256
GROUP = 32
LEVELS = 8
DIRS = 16
QUARTER = 128
TILES = 12
HALO = 24
LATE = 3
WINDOW = 32 + 2 * HALO
FACADES = 256

time_step = 0.12
viscosity = 0.2

MESH = pl.DeviceIdType.MESH
EXACT = lax.Precision.HIGHEST


def sine_matrix(n):
    k = np.arange(1, n + 1)
    return np.sqrt(2.0 / (n + 1)) * np.sin(np.pi * np.outer(k, k) / (n + 1))


def sweep_taps():
    along_x = 2.0 * np.cos(np.pi * np.arange(1, NX + 1) / (NX + 1))
    along_z = 2.0 * np.cos(np.pi * np.arange(1, NZ + 1) / (NZ + 1))
    own = (along_x[:, None] + along_z[None, :]) / 36.0
    side = 16.0 / 36.0
    width = ITERS
    taps = np.zeros((2 * width + 1, NX, NZ))
    for _ in range(ITERS):
        moved = own * taps
        moved[1:] += side * taps[:-1]
        moved[:-1] += side * taps[1:]
        moved[width] -= 1.0 / 36.0
        taps = moved
    taps = taps[width : width + ITERS]
    return np.stack([taps[:, :, QUARTER * k : QUARTER * (k + 1)] for k in range(4)])


def remote(src, dst, send, recv, to):
    return pltpu.make_async_remote_copy(
        src_ref=src, dst_ref=dst, send_sem=send, recv_sem=recv, device_id=to, device_id_type=MESH
    )


def shift_lanes(q, by):
    lane = lax.broadcasted_iota(jnp.int32, q.shape, 1)
    if by == 1:
        return jnp.where(lane == NZ - 1, 0.0, pltpu.roll(q, NZ - 1, 1))
    return jnp.where(lane == 0, 0.0, pltpu.roll(q, 1, 1))


def shift_x(q, by, edge):
    row = lax.broadcasted_iota(jnp.int32, q.shape, 0)
    if by == 1:
        return jnp.where(row == NX - 1, edge(q), pltpu.roll(q, NX - 1, 0))
    return jnp.where(row == 0, edge(q), pltpu.roll(q, 1, 0))


def copied(q):
    return q


def empty(q):
    return 0.0


def dot(a, b):
    return lax.dot_general(a, b, (((1,), (0,)), ((), ())), precision=EXACT, preferred_element_type=jnp.float32)


def bdot(a, b):
    return lax.dot_general(a, b, (((1,), (0,)), ((), ())), preferred_element_type=jnp.float32)


def thirds(x):
    high = x.astype(jnp.bfloat16)
    rest = x - high.astype(jnp.float32)
    middle = rest.astype(jnp.bfloat16)
    return high, middle, (rest - middle.astype(jnp.float32)).astype(jnp.bfloat16)


def dot_thirds(x, parts):
    n = x.shape[0]
    high, middle, low = thirds(x)
    a = bdot(jnp.concatenate([high, middle, low], axis=0), parts(0))
    b = bdot(jnp.concatenate([high, middle], axis=0), parts(1))
    c = bdot(high, parts(2))
    return a[:n] + ((a[n : 2 * n] + b[:n]) + (a[2 * n :] + (b[n:] + c)))


def kernel(
    vel, prec, rot, fcell_hbm, fown_hbm, fpan_hbm, farea_hbm, sz_hbm, taps_hbm, kx_hbm, kx10_hbm, sx_hbm,
    vel_hbm, pot_hbm, fout,
    vout,
    fcell, fown, fpan, farea, kx, kx10, sx,
    near_x, inlet, xl, wl,
    uext, pb, rr, col, pbuf, infl, ust, sz, taps, xh, win, ph, bk, phi, fterm, frecv,
    fa, fz, onpan, ohown,
    load_sem, go, s_u, r_u, s_p, r_p, s_r, r_r, s_t, r_t, s_i, r_i, s_x, r_x, s_l, r_l, s_b, r_b, s_f, r_f, s_c, r_c, l_p, out_sem,
):
    d = lax.axis_index("dir")
    s = lax.axis_index("space")
    zc = s // 4
    j = s % 4
    chip = s // 2
    is_owner = (s % 2 == 0) & (chip % 4 != 3)
    my_tile = chip - chip // 4
    owners = [2 * (t + t // 3) for t in range(TILES)]

    load_u = pltpu.make_async_copy(vel.at[0], uext.at[:, pl.ds(2, ROWS)], load_sem.at[0])
    load_u.start()
    load_s = pltpu.make_async_copy(sz_hbm, sz, load_sem.at[1])
    load_s.start()
    load_t = pltpu.make_async_copy(taps_hbm.at[j], taps, load_sem.at[2])
    load_t.start()
    lists = [(fcell_hbm, fcell), (fown_hbm, fown), (fpan_hbm, fpan), (farea_hbm, farea)]
    small = [(a, b.at[j]) for a, b in lists] + [(kx_hbm, kx), (kx10_hbm, kx10), (sx_hbm, sx)]
    small = [pltpu.make_async_copy(a, b, load_sem.at[3 + i]) for i, (a, b) in enumerate(small)]
    for load in small:
        load.start()

    barrier = pltpu.get_barrier_semaphore()

    @pl.when(d == 0)
    def _():
        for k in range(GROUP):
            pl.semaphore_signal(barrier, inc=1, device_id=(1, (s + k) % GROUP), device_id_type=MESH)
        pl.semaphore_wait(barrier, DIRS - 1)
        for c in range(3):
            for k in range(1, DIRS):
                remote(prec.at[0, c], pb.at[c], s_p.at[c, k], r_p.at[c], (k, s)).start()
        own = pltpu.make_async_copy(prec.at[0], pb, l_p)
        own.start()
        own.wait()
        pl.semaphore_wait(go, 1)

    @pl.when(d != 0)
    def _():
        pl.semaphore_signal(barrier, inc=1, device_id=(0, s), device_id_type=MESH)
        for k in range(1, GROUP):
            pl.semaphore_signal(barrier, inc=1, device_id=(d, (s + k) % GROUP), device_id_type=MESH)

    @pl.when(d == 1)
    def _():
        pl.semaphore_wait(barrier, 2 * GROUP - 1)
        pl.semaphore_signal(go, inc=1, device_id=(0, s), device_id_type=MESH)

    @pl.when(d > 1)
    def _():
        pl.semaphore_wait(barrier, GROUP - 1)

    for t in range(TILES):
        @pl.when(s != owners[t])
        def _(t=t):
            remote(rot.at[0, :, pl.ds(0, 128)], rr.at[pl.ds(8 * s, 8)], s_r, r_r, (d, owners[t])).start()

    up = (d, (s + 1) % GROUP)
    down = (d, (s + GROUP - 1) % GROUP)
    edges = [
        remote(vel.at[0, :, pl.ds(7, 1)], uext.at[:, pl.ds(1, 1)], s_u.at[0], r_u.at[0], up),
        remote(vel.at[0, pl.ds(1, 1), pl.ds(6, 1)], uext.at[pl.ds(1, 1), pl.ds(0, 1)], s_u.at[1], r_u.at[1], up),
        remote(vel.at[0, :, pl.ds(0, 1)], uext.at[:, pl.ds(10, 1)], s_u.at[2], r_u.at[2], down),
        remote(vel.at[0, pl.ds(1, 1), pl.ds(1, 1)], uext.at[pl.ds(1, 1), pl.ds(11, 1)], s_u.at[3], r_u.at[3], down),
    ]
    for edge in edges:
        edge.start()

    for dk in range(1, 4):
        for a, b in lists:
            remote(a, b.at[j], s_c, r_c, (d, 4 * zc + (j + dk) % 4)).start()

    for t in range(TILES):
        c, k = t // 4, t % 4

        @pl.when((d != 0) & (k == 0))
        def _(c=c):
            remote(prec.at[0, c], pb.at[c], s_p.at[c, 0], r_p.at[c], (0, s)).wait_recv()

        @pl.when(s != owners[t])
        def _(t=t, c=c, k=k):
            remote(pb.at[c, :, pl.ds(128 * k, 128)], col.at[pl.ds(8 * s, 8)], s_t, r_t, (d, owners[t])).start()

        @pl.when(s == owners[t])
        def _(t=t, c=c, k=k):
            col[pl.ds(pl.multiple_of(8 * s, 8), 8), :] = pb[c, :, 128 * k : 128 * (k + 1)]
            tile = pltpu.make_async_copy(rot.at[0, :, pl.ds(0, 128)], rr.at[pl.ds(8 * s, 8)], l_p)
            tile.start()
            tile.wait()

    @pl.when(is_owner)
    def _():
        part = pl.ds(0, 8 * (GROUP - 1))
        remote(rr.at[part], rr.at[part], s_r, r_r, (d, (s + 1) % GROUP)).wait_recv()
        q = rr[...] >> 9
        lane = lax.broadcasted_iota(jnp.int32, (NY, 128), 1)
        chosen = jnp.concatenate([jnp.where(q == lane, 1.0, 0.0), jnp.where(q - 128 == lane, 1.0, 0.0)], axis=1)
        chosen = chosen.astype(jnp.bfloat16)
        pbuf[0:8, :] = jnp.zeros((8, 128), jnp.float32)
        pbuf[NY : NY + 8, :] = jnp.zeros((8, 128), jnp.float32)
        remote(col.at[part], col.at[part], s_t, r_t, (d, (s + 1) % GROUP)).wait_recv()
        rows = bdot(chosen, jnp.concatenate(thirds(col[...]), axis=1))
        pbuf[4 : NY + 4, :] = rows[:, 0:128] + (rows[:, 128:256] + rows[:, 256:384])

        def send(i, carry):
            to = (s + 16 + ((i + 1) // 2) * (2 * (i % 2) - 1)) % GROUP
            remote(pbuf.at[pl.ds(8 * to, 16)], infl.at[my_tile], s_i, r_i, (d, to)).start()
            return carry

        lax.fori_loop(0, GROUP - 1, send, 0)
        infl[my_tile] = pbuf[pl.ds(pl.multiple_of(8 * s, 8), 16), :]

    load_u.wait()
    for load in small:
        load.wait()
    for edge in edges:
        edge.wait()
    blank = jnp.zeros((2, NX, NZ), jnp.float32)

    @pl.when(s == 0)
    def _():
        for c in range(3):
            uext[c, 0:2] = blank

    @pl.when(s == GROUP - 1)
    def _():
        for c in range(3):
            uext[c, 10:12] = blank

    def tentative(c, r):
        q = uext[c, r]
        yplus = uext[c, r + 1]
        yminus = uext[c, r - 1]
        xplus, xminus = shift_x(q, 1, copied), shift_x(q, -1, copied)
        zplus, zminus = shift_lanes(q, 1), shift_lanes(q, -1)
        lap = xplus + xminus + zplus + zminus + 16.0 * (yplus + yminus) - 36.0 * q
        advect = (
            uext[0, r] * (xplus - xminus) * 0.5
            + uext[1, r] * (yplus - yminus) * 2.0
            + uext[2, r] * (zplus - zminus) * 0.5
        )
        result = q + time_step * (viscosity * lap - advect)
        ust[c, r - 1] = jnp.where(lax.broadcasted_iota(jnp.int32, (NX, NZ), 0) < 2, 0.0, result)

    def row_y(r, carry):
        tentative(1, r)
        return carry

    def row_xz(r, carry):
        tentative(0, r)
        tentative(2, r)
        return carry

    lax.fori_loop(1, ROWS + 3, row_y, 0)
    lax.fori_loop(2, ROWS + 2, row_xz, 0)

    @pl.when(s == 0)
    def _():
        ust[1, 0] = jnp.zeros((NX, NZ), jnp.float32)

    @pl.when(s == GROUP - 1)
    def _():
        ust[1, ROWS + 1] = jnp.zeros((NX, NZ), jnp.float32)

    def row_div(r, carry):
        qx = ust[0, r + 1]
        qz = ust[2, r + 1]
        along_x = (shift_x(qx, 1, copied) - shift_x(qx, -1, copied)) * 0.5
        along_y = (ust[1, r + 2] - ust[1, r]) * 2.0
        along_z = (shift_lanes(qz, 1) - shift_lanes(qz, -1)) * 0.5
        phi[r] = along_x + along_y + along_z
        return carry

    lax.fori_loop(0, ROWS, row_div, 0)

    load_s.wait()
    modes = dot_thirds(dot(kx[...], phi[0:ROWS].reshape(ROWS * NX, NZ)), lambda i: sz[i])
    for k in range(4):
        xh[k] = modes[:, 128 * k : 128 * (k + 1)].reshape(ROWS, NX, QUARTER)

    above = 4 * ((zc + 1) % LEVELS)
    below = 4 * ((zc + LEVELS - 1) % LEVELS)

    def to_level(src, dst, send, recv):
        for dk in range(1, 4):
            k = (j + dk) % 4
            remote(src.at[k], dst(3 + j), send, recv, (d, 4 * zc + k)).start()

        @pl.when(j >= 1)
        def _():
            for k in range(4):
                remote(src.at[k], dst(j - 1), send, recv, (d, above + k)).start()

        @pl.when(j <= 2)
        def _():
            for k in range(4):
                remote(src.at[k], dst(7 + j), send, recv, (d, below + k)).start()

    to_level(xh, lambda b: win.at[pl.ds(8 * b, 8)], s_x, r_x)

    for c in range(3):
        for x in (1, 2):
            for r in range(ROWS + 4):
                near_x[c, x - 1, r + 2 : r + 3, :] = uext[c, r, x : x + 1, :]

    @pl.when(is_owner)
    def _():
        part = pl.ds(0, TILES - 1)
        remote(infl.at[part], infl.at[part], s_i, r_i, (d, (s + 1) % GROUP)).wait_recv()

    @pl.when(jnp.logical_not(is_owner))
    def _():
        remote(infl, infl, s_i, r_i, (d, (s + 1) % GROUP)).wait_recv()

    height = (2 * ROWS, NZ)
    row = lax.broadcasted_iota(jnp.int32, height, 0)
    outside = ((s == 0) & (row == 3)) | ((s == GROUP - 1) & (row == ROWS + 4))

    def y_next(q):
        return pltpu.roll(q, 2 * ROWS - 1, 0)

    def y_last(q):
        return pltpu.roll(q, 1, 0)

    at0 = [jnp.concatenate([infl[4 * c + k] for k in range(4)], axis=1) for c in range(3)]
    at1 = [near_x[c, 0] for c in range(3)]
    for x, (field, ahead, behind) in enumerate(((at0, at1, at0), (at1, [near_x[c, 1] for c in range(3)], at0))):
        for c in range(3):
            q, xplus, xminus = field[c], ahead[c], behind[c]
            yplus, yminus = y_next(q), y_last(q)
            zplus, zminus = shift_lanes(q, 1), shift_lanes(q, -1)
            lap = xplus + xminus + zplus + zminus + 16.0 * (yplus + yminus) - 36.0 * q
            advect = (
                field[0] * (xplus - xminus) * 0.5
                + field[1] * (yplus - yminus) * 2.0
                + field[2] * (zplus - zminus) * 0.5
            )
            result = q + time_step * (viscosity * lap - advect)
            inlet[x, c] = jnp.where(outside, 0.0, result) if c == 1 else result

    def beside(x):
        qy, qz = inlet[x, 1], inlet[x, 2]
        return (y_next(qy) - y_last(qy)) * 2.0 + (shift_lanes(qz, 1) - shift_lanes(qz, -1)) * 0.5

    v0, v1 = inlet[0, 0], inlet[1, 0]
    parts = [(v1 - v0) * 0.5 + beside(0), beside(1) - v0 * 0.5, v1 * -0.5]
    rows = [part[4:12] for part in parts] + [jnp.zeros((ROWS, NZ), jnp.float32)]
    late = dot_thirds(jnp.concatenate(rows, axis=0), lambda i: sz[i])
    for k in range(4):
        xl[k] = late[0 : LATE * ROWS, 128 * k : 128 * (k + 1)]
    to_level(xl, lambda b: wl.at[b], s_l, r_l)

    for x in range(2):
        for c in range(3):
            for r in range(ROWS):
                ust[c, r + 1, x : x + 1, :] = inlet[x, c, r + 4 : r + 5, :]

    remote(xl.at[0], xl.at[0], s_c, r_c, up).wait_recv()
    wide = lax.broadcasted_iota(jnp.int32, (FACADES, 128), 1)
    tall = lax.broadcasted_iota(jnp.int32, (FACADES, NZ), 1)
    mine = pl.ds(pl.multiple_of(128 * j, 128), 128)

    def prepare(q, carry):
        cell = jnp.transpose(jnp.broadcast_to(fcell[q], (8, FACADES)))[:, 0:1]
        panel = jnp.transpose(jnp.broadcast_to(fpan[q], (8, FACADES)))[:, 0:1]
        area = jnp.transpose(jnp.broadcast_to(farea[q], (8, FACADES)))[:, 0:1]
        fa[q] = dot(jnp.where((cell >> 9) == wide, 1.0, 0.0), kx[...])
        at = jnp.where((cell & 511) == tall, 1.0, 0.0).astype(jnp.bfloat16)
        fz[q] = (bdot(at, sz[0, :, mine]) + (bdot(at, sz[1, :, mine]) + bdot(at, sz[2, :, mine]))) * area
        onpan[q] = jnp.where(panel == wide, 1.0, 0.0)
        ohown[q] = jnp.where(lax.broadcasted_iota(jnp.int32, (GROUP, FACADES), 0) == fown[q], 1.0, 0.0)
        return carry

    lax.fori_loop(0, 4, prepare, 0)

    win[pl.ds(HALO + 8 * j, 8)] = xh[j]
    wl[3 + j] = xl[j]
    load_t.wait()
    others = pl.ds(0, WINDOW - 8)
    remote(win.at[others], win.at[others], s_x, r_x, (d, (s + 1) % GROUP)).wait_recv()
    nine = pl.ds(0, 9)
    remote(wl.at[nine], wl.at[nine], s_l, r_l, (d, (s + 1) % GROUP)).wait_recv()

    def join(b, carry):
        block = wl[b]
        for r in range(ROWS):
            total = win[8 * b + r]
            for x in range(LATE):
                total = total + jnp.broadcast_to(block[8 * x + r : 8 * x + r + 1, :], (NX, QUARTER)) * sx[x]
            win[8 * b + r] = total
        return carry

    lax.fori_loop(0, WINDOW // 8, join, 0)

    @pl.when(zc == 0)
    def _():
        win[HALO - 1] = jnp.zeros((NX, QUARTER), jnp.float32)
        for i in range(1, ITERS):
            win[HALO - 1 - i] = -win[HALO - 1 + i]

    @pl.when(zc == LEVELS - 1)
    def _():
        win[HALO + 32] = jnp.zeros((NX, QUARTER), jnp.float32)
        for i in range(1, ITERS):
            win[HALO + 32 + i] = -win[HALO + 32 - i]

    backs = []
    for dk in (2, 3, 1, 0):
        first = 8 * (j ^ dk)

        def filter_pair(y, carry, first=first, dk=dk):
            at = first + 2 * y + HALO - 1
            near = {0: win[at], 1: win[at + 1]}
            one, two = taps[0] * near[0], taps[0] * near[1]
            for i in range(1, ITERS):
                near[1 + i], near[-i] = win[at + 1 + i], win[at - i]
                tap = taps[i]
                one = one + tap * (near[i] + near[-i])
                two = two + tap * (near[1 + i] + near[1 - i])
            ph[dk, 2 * y] = one
            ph[dk, 2 * y + 1] = two
            return carry

        lax.fori_loop(0, ROWS // 2 + 1, filter_pair, 0)
        if dk:
            back = remote(ph.at[dk], bk.at[dk], s_b.at[dk], r_b.at[dk], (d, 4 * zc + (j ^ dk)))
            back.start()
            backs.append(back)

    terms = jnp.zeros((GROUP, PAN_DEV), jnp.float32)
    for dk in range(4):
        q = j ^ dk
        lines = dot(fa[q], ph[dk, 1 : ROWS + 1].reshape(ROWS * NX, QUARTER))
        value = jnp.sum(lines * fz[q], axis=1, keepdims=True)
        terms = terms + dot(ohown[q], onpan[q] * value)
    for o in range(GROUP):
        fterm[o] = terms[o : o + 1, :]

    def send_terms(i, carry):
        to = (s + 16 + ((i + 1) // 2) * (2 * (i % 2) - 1)) % GROUP
        remote(fterm.at[to], frecv.at[s], s_f, r_f, (d, to)).start()
        return carry

    lax.fori_loop(0, GROUP - 1, send_terms, 0)
    frecv[s] = fterm[s]

    def quarter(block, k):
        rows = pl.ds(pl.multiple_of(128 * k, 128), 128)
        return dot_thirds(block.reshape(10 * NX, QUARTER), lambda i: sz[i, rows, :])

    spread = quarter(ph[0], j)
    for dk in (1, 2, 3):
        arrived = backs[(2, 3, 1).index(dk)]
        arrived.wait_recv()
        spread = spread + quarter(bk[dk], j ^ dk)
    phi[...] = dot(kx10[...], spread).reshape(10, NX, NZ)

    @pl.when(s == 0)
    def _():
        phi[0] = jnp.zeros((NX, NZ), jnp.float32)

    @pl.when(s == GROUP - 1)
    def _():
        phi[ROWS + 1] = jnp.zeros((NX, NZ), jnp.float32)

    def row_out(r, carry):
        q = phi[r + 1]
        vout[0, r] = ust[0, r + 1] - (shift_x(q, 1, empty) - shift_x(q, -1, empty)) * 0.5
        vout[1, r] = ust[1, r + 1] - (phi[r + 2] - phi[r]) * 2.0
        vout[2, r] = ust[2, r + 1] - (shift_lanes(q, 1) - shift_lanes(q, -1)) * 0.5
        return carry

    lax.fori_loop(0, ROWS, row_out, 0)
    outs = [
        pltpu.make_async_copy(phi.at[pl.ds(1, ROWS)], pot_hbm.at[0], out_sem.at[0]),
        pltpu.make_async_copy(vout, vel_hbm.at[0], out_sem.at[1]),
    ]
    for out in outs:
        out.start()

    @pl.when(d == 0)
    def _():
        for c in range(3):
            for k in range(1, DIRS):
                remote(prec.at[0, c], pb.at[c], s_p.at[c, k], r_p.at[c], (k, s)).wait_send()

    eight = pl.ds(0, 8 * (TILES - 1))

    remote(xl.at[0], xl.at[0], s_c, r_c, up).wait_send()
    remote(rr.at[eight], rr.at[eight], s_r, r_r, up).wait_send()
    remote(col.at[eight], col.at[eight], s_t, r_t, up).wait_send()

    @pl.when(jnp.logical_not(is_owner))
    def _():
        remote(rr.at[pl.ds(0, 8)], rr.at[pl.ds(0, 8)], s_r, r_r, up).wait_send()
        remote(col.at[pl.ds(0, 8)], col.at[pl.ds(0, 8)], s_t, r_t, up).wait_send()

    @pl.when(is_owner)
    def _():
        sent = pl.ds(0, GROUP - 1)
        remote(win.at[sent], win.at[sent], s_i, r_i, up).wait_send()

    @pl.when((j == 0) | (j == 3))
    def _():
        remote(win.at[pl.ds(0, 56)], win.at[pl.ds(0, 56)], s_x, r_x, up).wait_send()
        remote(wl.at[pl.ds(0, 7)], wl.at[pl.ds(0, 7)], s_l, r_l, up).wait_send()

    @pl.when((j == 1) | (j == 2))
    def _():
        remote(win, win, s_x, r_x, up).wait_send()
        remote(win.at[pl.ds(0, 8)], win.at[pl.ds(0, 8)], s_x, r_x, up).wait_send()
        remote(wl, wl, s_l, r_l, up).wait_send()
        remote(wl.at[0], wl.at[0], s_l, r_l, up).wait_send()

    for back in backs:
        back.wait_send()
    rest = pl.ds(0, GROUP - 1)
    remote(frecv.at[rest], frecv.at[rest], s_f, r_f, up).wait()
    fout[...] = jnp.sum(frecv[...], axis=0)
    for out in outs:
        out.wait()


def write_out(vel, pot, force, vel_out, pot_out, force_out, vbuf, pbuf, fbuf, into, out):
    half = ROWS // 2
    parts = [
        (vel.at[0, c, pl.ds(r, half)], vbuf.at[c, pl.ds(r, half)], vel_out.at[0, c, pl.ds(r, half)])
        for c in range(3)
        for r in (0, half)
    ]
    parts += [(pot.at[0, pl.ds(r, half)], pbuf.at[pl.ds(r, half)], pot_out.at[0, pl.ds(r, half)]) for r in (0, half)]
    parts.append((force, fbuf, force_out))
    loads = [pltpu.make_async_copy(a, b, into.at[i]) for i, (a, b, _) in enumerate(parts)]
    stores = [pltpu.make_async_copy(b, c, out.at[i]) for i, (_, b, c) in enumerate(parts)]
    for load in loads:
        load.start()
    for load, store in zip(loads, stores):
        load.wait()
        store.start()
    for store in stores:
        store.wait()


def body(velocity, precursor, rot_map, facade_cell, facade_owner, facade_panel, facade_area):
    f32 = jnp.float32
    across = sine_matrix(NX)
    constants = [
        jnp.stack(thirds(jnp.asarray(sine_matrix(NZ), f32))),
        jnp.asarray(sweep_taps(), f32),
        jnp.asarray(np.kron(np.eye(ROWS), across), f32),
        jnp.asarray(np.kron(np.eye(ROWS + 2), across), f32),
        jnp.asarray(np.broadcast_to(across[:LATE, :, None], (LATE, NX, QUARTER)), f32),
    ]
    far = pl.BlockSpec(memory_space=pltpu.HBM)
    near = pl.BlockSpec(memory_space=pltpu.VMEM)
    dma = pltpu.SemaphoreType.DMA
    result = pl.pallas_call(
        kernel,
        out_shape=(
            jax.ShapeDtypeStruct((1, 3, ROWS, NX, NZ), f32),
            jax.ShapeDtypeStruct((1, ROWS, NX, NZ), f32),
            jax.ShapeDtypeStruct((1, PAN_DEV), f32),
        ),
        in_specs=[far] * 12,
        out_specs=(far, far, near),
        scratch_shapes=[
            pltpu.VMEM((3, ROWS, NX, NZ), f32),
            pltpu.VMEM((4, 1, FACADES), jnp.int32),
            pltpu.VMEM((4, 1, FACADES), jnp.int32),
            pltpu.VMEM((4, 1, FACADES), jnp.int32),
            pltpu.VMEM((4, 1, FACADES), f32),
            pltpu.VMEM((ROWS * NX, ROWS * NX), f32),
            pltpu.VMEM(((ROWS + 2) * NX, (ROWS + 2) * NX), f32),
            pltpu.VMEM((LATE, NX, QUARTER), f32),
            pltpu.VMEM((3, 2, 2 * ROWS, NZ), f32),
            pltpu.VMEM((2, 3, 2 * ROWS, NZ), f32),
            pltpu.VMEM((4, LATE * ROWS, QUARTER), f32),
            pltpu.VMEM((WINDOW // 8, LATE * ROWS, QUARTER), f32),
            pltpu.VMEM((3, ROWS + 4, NX, NZ), f32),
            pltpu.VMEM((3, ROWS, NZ), f32),
            pltpu.VMEM((NY, 128), jnp.int32),
            pltpu.VMEM((NY, 128), f32),
            pltpu.VMEM((NY + 8, 128), f32),
            pltpu.VMEM((TILES, 16, 128), f32),
            pltpu.VMEM((3, ROWS + 2, NX, NZ), f32),
            pltpu.VMEM((3, NZ, NZ), jnp.bfloat16),
            pltpu.VMEM((ITERS, NX, QUARTER), f32),
            pltpu.VMEM((4, ROWS, NX, QUARTER), f32),
            pltpu.VMEM((WINDOW, NX, QUARTER), f32),
            pltpu.VMEM((4, ROWS + 2, NX, QUARTER), f32),
            pltpu.VMEM((4, ROWS + 2, NX, QUARTER), f32),
            pltpu.VMEM((ROWS + 2, NX, NZ), f32),
            pltpu.VMEM((GROUP, 1, PAN_DEV), f32),
            pltpu.VMEM((GROUP, 1, PAN_DEV), f32),
            pltpu.VMEM((4, FACADES, 128), f32),
            pltpu.VMEM((4, FACADES, 128), f32),
            pltpu.VMEM((4, FACADES, 128), f32),
            pltpu.VMEM((4, GROUP, FACADES), f32),
            dma((10,)), pltpu.SemaphoreType.REGULAR, dma((4,)), dma((4,)), dma((3, DIRS)),
            dma((3,)), dma, dma, dma, dma, dma, dma, dma, dma, dma, dma, dma((4,)), dma((4,)), dma, dma, dma, dma, dma, dma((2,)),
        ],
        compiler_params=pltpu.CompilerParams(
            collective_id=0, has_side_effects=True, vmem_limit_bytes=60 << 20
        ),
    )(
        velocity, precursor, rot_map, facade_cell, facade_owner.reshape(1, FACADES), facade_panel, facade_area, *constants
    )
    return pl.pallas_call(
        write_out,
        out_shape=[jax.ShapeDtypeStruct(x.shape, x.dtype) for x in result],
        in_specs=[far] * 3,
        out_specs=[far] * 3,
        scratch_shapes=[
            pltpu.VMEM((3, ROWS, NX, NZ), f32),
            pltpu.VMEM((ROWS, NX, NZ), f32),
            pltpu.VMEM((1, PAN_DEV), f32),
            dma((9,)),
            dma((9,)),
        ],
        compiler_params=pltpu.CompilerParams(vmem_limit_bytes=60 << 20),
    )(*result)


def solution(mesh):
    return jax.shard_map(
        body,
        mesh=mesh,
        in_specs=(
            P("dir", None, "space", None, None),
            P("dir", None, "space", None),
            P("dir", "space", None),
            P("dir", "space"),
            P("dir", "space", None),
            P("dir", "space"),
            P("dir", "space"),
        ),
        out_specs=(
            P("dir", None, "space", None, None),
            P("dir", "space", None, None),
            P("dir", "space"),
        ),
        check_vma=False,
    )
```
